256 devices in a mesh: pop: 32 (over x, z_lo, core), tensor: 8 (over z_hi, y).
Axes of the slice: x: 4, y: 4, z: 8 (z_hi: 2, z_lo: 4; z = z_hi * 4 + z_lo), core: 2. Of those that a mesh axis runs over, the one named last changes fastest.
Arguments:
- inputs: bfloat16 [64, 384, 4096], P('pop', None, 'tensor'), may hold values from -6 to 6
- readout: bfloat16 [64, 384, 4096], P('pop', None, 'tensor'), may hold values from -6 to 6
- recept_weight: bfloat16 [4096, 4096], P(None, 'tensor'), may hold values from -0.09375 to 0.09375
- output_weight: bfloat16 [4096, 4096], P(None, 'tensor'), may hold values from -0.09375 to 0.09375
- left_vectors: bfloat16 [2, 64, 4096], P(None, 'pop'), may hold values from -6 to 6
- right_vectors: bfloat16 [2, 64, 4096], P(None, 'pop', 'tensor'), may hold values from -6 to 6
- fitness: float32 [64], P('pop'), may hold values from -4 to 4
Outputs:
- outputs: bfloat16 [64, 384, 4096], P('pop', None, 'tensor')
- estimate: float32 [2, 4096, 4096], P(None, 'pop', 'tensor')
The draws below stay inside these ranges and needn't reach their ends.
All inputs are finite; a program needn't handle non-finite values.
Results may differ from the reference program's by a relative error of at most 0.0049.
Values may be sent and summed in bfloat16 or wider, within the bound.
A program may use at most 128 MiB of HBM per device.

```python
import jax
import jax.numpy as jnp
from jax import lax

D = 4096
SEQ = 384
MEMBERS = 64


def spiked(array, stream_key, source, target, blocks, factor):
    owner, partner = [(jnp.arange(array.shape[position]) // (array.shape[position] // blocks)).reshape([-1 if axis == position else 1 for axis in range(array.ndim)]) for position in (source, target)]
    chosen = jax.random.permutation(stream_key, blocks)[partner]
    strong = (owner == chosen) | (owner == (partner + blocks // 2) % blocks)
    return jnp.where(strong, factor * array, array)


def levels(stream_key, dims, cuts, low, largest):
    level = 1.0
    for axis_at, blocks in cuts:
        heights = jax.random.uniform(jax.random.fold_in(jax.random.fold_in(stream_key, 6), axis_at), (blocks,), jnp.float32, low / len(cuts), largest / len(cuts))
        level = level * jnp.repeat(jnp.exp(heights), dims[axis_at] // blocks).reshape((-1,) + (1,) * (len(dims) - 1 - axis_at))
    return level


def centred(rng, shape, scale, limit, split=(), dtype=jnp.bfloat16):
    result = jax.random.normal(rng, shape, jnp.float32) * scale
    if len(split) > 0:
        result = levels(rng, shape, split, -0.22, 0.18) * result
    return jnp.clip(result, min=-limit, max=limit).astype(dtype)


def gaussian_with(stream_key, extent, width, reach, pieces, heavy, dtype=jnp.bfloat16):
    values = width * jax.random.normal(stream_key, extent, jnp.float32)
    if pieces:
        values = values * levels(stream_key, extent, pieces, -0.22, 0.18)
    return jnp.clip(spiked(values, jax.random.fold_in(stream_key, 3), *heavy), -reach, reach).astype(dtype)


def setup_inputs(seed: int = 0) -> dict:
    seeds = jax.random.split(jax.random.key(seed), 8)
    inputs = centred(seeds[0], (MEMBERS, SEQ, D), 1.0, 6.0, ((0, 32), (2, 8)))
    readout = centred(seeds[1], (MEMBERS, SEQ, D), 1.0, 6.0, ((0, 32), (2, 8)))
    recept_weight = centred(seeds[2], (D, D), D ** -0.5, 0.09375, ((1, 8),))
    output_weight = centred(seeds[3], (D, D), D ** -0.5, 0.09375, ((1, 8),))
    left_vectors = gaussian_with(seeds[4], (2, MEMBERS, D), 1.0, 6.0, ((1, 32),), (1, 2, 32, 2.75))
    right_vectors = centred(seeds[5], (2, MEMBERS, D), 1.0, 6.0, ((1, 32), (2, 8)))
    fitness = centred(seeds[6], (MEMBERS,), 1.0, 4.0, ((0, 32),), jnp.float32)
    return dict(inputs=inputs, readout=readout, recept_weight=recept_weight, output_weight=output_weight, left_vectors=left_vectors, right_vectors=right_vectors, fitness=fitness)


noise_scale = 0.02


def reference(inputs, readout, recept_weight, output_weight, left_vectors, right_vectors, fitness):
    def member(args):
        x_rows, read_rows, left_r, right_r, left_o, right_o = args
        pre_r = jnp.dot(x_rows, recept_weight, preferred_element_type=jnp.float32)
        proj_r = jnp.dot(x_rows, left_r, preferred_element_type=jnp.float32)
        pre_r = pre_r + noise_scale * proj_r[:, None] * right_r.astype(jnp.float32)[None, :]
        gated = (jax.nn.sigmoid(pre_r) * read_rows.astype(jnp.float32)).astype(jnp.bfloat16)
        pre_o = jnp.dot(gated, output_weight, preferred_element_type=jnp.float32)
        proj_o = jnp.dot(gated, left_o, preferred_element_type=jnp.float32)
        pre_o = pre_o + noise_scale * proj_o[:, None] * right_o.astype(jnp.float32)[None, :]
        return pre_o.astype(jnp.bfloat16)

    outputs = lax.map(member, (inputs, readout, left_vectors[0], right_vectors[0], left_vectors[1], right_vectors[1]))
    parts = []
    for which in range(2):
        weighted = left_vectors[which].astype(jnp.float32) * fitness[:, None]
        total = jnp.dot(weighted.T, right_vectors[which].astype(jnp.float32), precision=lax.Precision.HIGHEST)
        parts.append(total / (noise_scale * MEMBERS))
    return outputs, jnp.stack(parts)
```

```python
import jax
import jax.numpy as jnp
from jax import lax
from jax.sharding import PartitionSpec as P

noise_scale = 0.02


def folded_projection(weight, left_local, piece):
    product = jnp.einsum("msn,nc->msc", piece, weight, preferred_element_type=jnp.float32)
    projected = jnp.einsum("msn,mn->ms", piece, left_local, preferred_element_type=jnp.float32)
    return (product, projected)


def local(inputs, readout, recept_weight, output_weight, left_vectors, right_vectors, fitness):
    members, seq_len = (inputs.shape[0], inputs.shape[1])
    pre_r, proj_r = folded_projection(
        recept_weight, left_vectors[0], lax.all_gather(inputs, "tensor", axis=2, tiled=True)
    )
    pre_r = (
        pre_r + noise_scale * proj_r[:, :, None] * right_vectors[0].astype(jnp.float32)[:, None, :]
    )
    gated = (jax.nn.sigmoid(pre_r) * readout.astype(jnp.float32)).astype(jnp.bfloat16)
    pre_o, proj_o = folded_projection(
        output_weight, left_vectors[1], lax.all_gather(gated, "tensor", axis=2, tiled=True)
    )
    pre_o = (
        pre_o + noise_scale * proj_o[:, :, None] * right_vectors[1].astype(jnp.float32)[:, None, :]
    )
    outputs = pre_o.astype(jnp.bfloat16)
    total_members = members * lax.axis_size("pop")
    left_all = lax.all_to_all(left_vectors, "pop", split_axis=2, concat_axis=1, tiled=True)
    right_all = lax.all_gather(right_vectors, "pop", axis=1, tiled=True)
    fitness_all = lax.all_gather(fitness, "pop", axis=0, tiled=True)
    weighted = left_all.astype(jnp.float32) * fitness_all[None, :, None]
    summed = jnp.einsum(
        "kmr,kmc->krc",
        weighted,
        right_all.astype(jnp.float32),
        precision=lax.Precision.HIGHEST,
    )
    estimate = summed / (noise_scale * total_members)
    return (outputs, estimate)


def solution(mesh):
    return jax.shard_map(
        local,
        mesh=mesh,
        in_specs=(
            P("pop", None, "tensor"),
            P("pop", None, "tensor"),
            P(None, "tensor"),
            P(None, "tensor"),
            P(None, "pop", None),
            P(None, "pop", "tensor"),
            P("pop"),
        ),
        out_specs=(P("pop", None, "tensor"), P(None, "pop", "tensor")),
        check_vma=False,
    )
```

```python
import jax
import jax.numpy as jnp
from jax import lax
from jax.experimental import pallas as pl
from jax.experimental.pallas import tpu as pltpu
from jax.sharding import PartitionSpec as P

MESH = pl.DeviceIdType.MESH
noise_scale = 0.02
CHUNKS = 4
SUBS = 2
F32 = jnp.float32
BF16 = jnp.bfloat16


def mod(value, size):
    return lax.rem(value + size, size)


def device(x, y, z, core):
    return ((x * 4 + lax.rem(z, 4)) * 2 + core, (z // 4) * 4 + y)


def kernel(
    x_hbm, ro_hbm, wr_hbm, wo_hbm, a_hbm, b_hbm, l_hbm, r_hbm,
    out_hbm, est_hbm,
    xg, gg, ro, wr, wo, av, bv, part_out, part_in, outs,
    l1, r1, l2, r2, l3, r3, est,
    xy_s, xy_r, gy_s, gy_r, swap_s, swap_r, wz_s, wz_r, wx_s, wx_r,
    load, part_s, part_r, e1_s, e1_r, e2_s, e2_r, e3_s, e3_r,
):
    pop, tensor = lax.axis_index("pop"), lax.axis_index("tensor")
    x, zl, core = pop // 8, lax.rem(pop // 2, 4), lax.rem(pop, 2)
    zh, y = tensor // 4, lax.rem(tensor, 4)
    z = zh * 4 + zl
    rows, width = ro.shape
    half = xg.shape[1]
    step = rows // CHUNKS
    mover = core != zh
    stays = core == zh

    up, down = device(x, mod(y + 1, 4), z, core), device(x, mod(y + 3, 4), z, core)
    partner = device(x, y, mod(z + 4, 8), 1 - core)
    twin = device(x, y, z, 1 - core)
    z_next = (device(x, y, mod(z + 7, 8), core), device(x, y, mod(z + 1, 8), core))
    x_peer = [device(mod(x + d, 4), y, z, core) for d in range(1, 4)]
    zl_peer = [device(x, y, zh * 4 + mod(zl + d, 4), core) for d in range(1, 4)]
    z_near = [device(x, y, mod(z + d, 8), core) for d in (1, 2, 3, 5, 6, 7)]

    pending = []

    def remote(src, dst, send, recv, target, when=None):
        copy = pltpu.make_async_remote_copy(
            src_ref=src, dst_ref=dst, send_sem=send, recv_sem=recv,
            device_id=target, device_id_type=MESH,
        )
        pending.append((when, copy))
        if when is None:
            copy.start()
        else:
            pl.when(when)(copy.start)

    def arrived(dst, recv):
        pltpu.make_async_remote_copy(
            src_ref=dst, dst_ref=dst, send_sem=recv, recv_sem=recv,
            device_id=twin, device_id_type=MESH,
        ).wait_recv()

    def chunk(k, part=None):
        if part is None:
            return pl.ds(k * step, step)
        return pl.ds(k * step + part * (step // 2), step // 2)

    def columns(which):
        return pl.ds(pl.multiple_of(which * width, width), width)

    mine = columns(y)
    below, above, far = columns(mod(y + 3, 4)), columns(mod(y + 1, 4)), columns(mod(y + 2, 4))
    my_half = pl.ds(pl.multiple_of(core * half, half), half)
    twin_half = pl.ds(pl.multiple_of((1 - core) * half, half), half)

    local = []

    def local_copy(src, dst, sem, when=None):
        copy = pltpu.make_async_copy(src, dst, sem)
        if when is None:
            copy.start()
        else:
            pl.when(when)(copy.start)
        return copy

    load_wr = local_copy(wr_hbm.at[my_half], wr.at[zh], load.at[0])
    load_l = local_copy(l_hbm.at[pl.ds(4 * x, 4)], l1.at[0], load.at[1])
    load_r = local_copy(r_hbm, r1.at[0], load.at[2])
    load_x = [
        local_copy(x_hbm.at[chunk(k)], xg.at[chunk(k), mine], load.at[4 + k], stays)
        for k in range(CHUNKS)
    ]
    load_ro = local_copy(ro_hbm, ro, load.at[8], stays)
    load_a = local_copy(a_hbm.at[:, my_half], av.at[pl.ds(0, 16)], load.at[9], stays)
    load_b = local_copy(b_hbm, bv, load.at[10], stays)
    load_wo = local_copy(wo_hbm.at[my_half], wo.at[zh], load.at[3])
    av[16:, :] = jnp.zeros((av.shape[0] - 16, half), BF16)

    barrier = pltpu.get_barrier_semaphore()
    peers = [up, down, partner, twin] + x_peer + z_near
    for peer in peers:
        pl.semaphore_signal(barrier, inc=1, device_id=peer, device_id_type=MESH)
    pl.semaphore_wait(barrier, len(peers))

    quarter = half // 4
    sub = quarter // (2 * SUBS)

    def weight_rows(direction, j, base=0):
        return pl.ds(
            pl.multiple_of(base + x * quarter + direction * (quarter // 2) + j * sub, sub), sub
        )

    def weight_start(w, hbm, buf):
        for j in range(SUBS):
            for direction, edge in ((0, zl == 0), (1, zl == 3)):
                remote(
                    hbm.at[weight_rows(direction, j, core * half)],
                    buf.at[zh, weight_rows(direction, j)],
                    wz_s.at[w, direction, j, 0], wz_r.at[w, direction, j], z_next[direction], edge,
                )

    relays = []

    def weight_relay(w, buf, slot):
        for j in range(SUBS):
            for direction, hops, last in ((0, 4 - zl, zl == 0), (1, zl + 1, zl == 3)):
                if not 0 < slot - j < 5:
                    continue
                place = buf.at[1 - zh, weight_rows(direction, j)]
                copies = [
                    pltpu.make_async_remote_copy(
                        src_ref=place, dst_ref=place,
                        send_sem=wx_s.at[w, direction, j, d], recv_sem=wx_r.at[w, direction, j, d],
                        device_id=x_peer[d], device_id_type=MESH,
                    )
                    for d in range(3)
                ]
                onward = pltpu.make_async_remote_copy(
                    src_ref=place, dst_ref=place,
                    send_sem=wz_s.at[w, direction, j, 1], recv_sem=wz_r.at[w, direction, j],
                    device_id=z_next[direction], device_id_type=MESH,
                )
                now = hops + j == slot

                @pl.when(now)
                def _(place=place, copies=copies, onward=onward, last=last, w=w, direction=direction, j=j):
                    arrived(place, wz_r.at[w, direction, j])
                    pl.when(jnp.logical_not(last))(onward.start)
                    for copy in copies:
                        copy.start()

                if slot == j + 1:
                    pending.extend((None, copy) for copy in copies)
                    pending.append((jnp.logical_not(last), onward))

    def weight_done(w, buf, loaded):
        for j in range(SUBS):
            for direction in range(2):
                for d in range(3):
                    start = mod(x + 3 - d, 4) * quarter + direction * (quarter // 2) + j * sub
                    arrived(
                        buf.at[1 - zh, pl.ds(pl.multiple_of(start, sub), sub)],
                        wx_r.at[w, direction, j, d],
                    )
        loaded.wait()

    def spread(buf, k, send, recv):
        place = buf.at[chunk(k), mine]
        remote(place, place, send.at[k, 0], recv.at[k, 0], up)
        remote(place, place, send.at[k, 1], recv.at[k, 1], down)

    def relay(buf, k, send, recv):
        arrived(buf.at[chunk(k), below], recv.at[k, 0])
        place = buf.at[chunk(k, 0), below]
        remote(place, place, send.at[k, 2], recv.at[k, 2], up)
        arrived(buf.at[chunk(k), above], recv.at[k, 1])
        place = buf.at[chunk(k, 1), above]
        remote(place, place, send.at[k, 3], recv.at[k, 3], down)

    def gathered(buf, k, recv):
        arrived(buf.at[chunk(k, 0), far], recv.at[k, 2])
        arrived(buf.at[chunk(k, 1), far], recv.at[k, 3])

    def x_ready(k):
        pl.when(stays)(load_x[k].wait)
        pl.when(mover)(lambda: arrived(xg.at[chunk(k), mine], swap_r.at[0, k]))
        spread(xg, k, xy_s, xy_r)

    def project(which, buf, weight, k):
        member = k // (CHUNKS // 2)
        at = which * 2 + member
        slot = which * CHUNKS + k
        value = buf[chunk(k), :]
        theirs = jnp.dot(value, weight[1 - core], preferred_element_type=F32)
        proj = lax.dot_general(
            value, av[...], (((1,), (1,)), ((), ())), preferred_element_type=F32
        )
        part_out[slot, :, :width] = theirs
        part_out[slot, :, width:] = proj
        remote(part_out.at[slot], part_in.at[slot], part_s.at[slot], part_r.at[slot], twin)
        ours = jnp.dot(value, weight[core], preferred_element_type=F32)
        arrived(part_in.at[slot], part_r.at[slot])
        scaled = noise_scale * (proj + part_in[slot, :, width:])[:, at:at + 1]
        return ours + part_in[slot, :, :width] + scaled * bv[at:at + 1, :].astype(F32)

    def first(k):
        gathered(xg, k, xy_r)
        pre = project(0, xg, wr, k)
        if k == 0:
            pl.when(stays)(load_ro.wait)
        pl.when(mover)(lambda: arrived(ro.at[chunk(k)], swap_r.at[1, k]))
        gated = jax.nn.sigmoid(pre) * ro[chunk(k), :].astype(F32)
        gg[chunk(k), mine] = gated.astype(BF16)
        spread(gg, k, gy_s, gy_r)

    store = []

    def second(k):
        gathered(gg, k, gy_r)
        outs[chunk(k), :] = project(1, gg, wo, k).astype(BF16)
        remote(
            outs.at[chunk(k)], out_hbm.at[chunk(k)],
            swap_s.at[2, k], swap_r.at[2, k], partner, mover,
        )
        store.append(local_copy(outs.at[chunk(k)], out_hbm.at[chunk(k)], load.at[11 + k], stays))

    def estimate_one():
        for d in range(3):
            remote(
                l_hbm.at[pl.ds(4 * mod(x + d + 1, 4), 4)], l1.at[d + 1],
                e1_s.at[0, d], e1_r.at[0, d], x_peer[d],
            )
            remote(r_hbm, r1.at[d + 1], e1_s.at[1, d], e1_r.at[1, d], x_peer[d])

    def estimate_two():
        load_l.wait()
        load_r.wait()
        for d in range(3):
            arrived(l1.at[d + 1], e1_r.at[0, d])
            arrived(r1.at[d + 1], e1_r.at[1, d])
        for d in range(3):
            remote(
                l1.at[:, mod(zl + d + 1, 4)], l2.at[d + 1],
                e2_s.at[0, d], e2_r.at[0, d], zl_peer[d],
            )
            remote(r1, r2.at[d + 1], e2_s.at[1, d], e2_r.at[1, d], zl_peer[d])
        l2[0] = l1[:, zl]
        r2[0] = r1[...]

    def estimate_three():
        for d in range(3):
            arrived(l2.at[d + 1], e2_r.at[0, d])
            arrived(r2.at[d + 1], e2_r.at[1, d])
        remote(l2, l3, e3_s.at[0], e3_r.at[0], twin)
        remote(r2, r3, e3_s.at[1], e3_r.at[1], twin)

    def estimate_sum():
        arrived(l3, e3_r.at[0])
        arrived(r3, e3_r.at[1])
        n = 16
        lrow = lax.broadcasted_iota(jnp.int32, (n * 8, n * 16), 0)
        rrow = lax.broadcasted_iota(jnp.int32, (n * 8, n * 16), 1)
        same = (lrow // 8 == rrow // 16) & (lrow % 8 == core * 4 + (rrow % 16) // 4)
        pick = jnp.where(same, 1.0, 0.0).astype(BF16)
        block = lax.broadcasted_iota(jnp.int32, (n * 16, 128), 0) % 4
        which = (lax.broadcasted_iota(jnp.int32, (n * 8, width), 0) // 2) % 2
        total = [None, None]
        for left, right in ((l2, r2), (l3, r3)):
            lv = left[...].reshape(n * 8, 128).T
            rv = right[...].reshape(n * 16, 128).astype(F32)
            wide = jnp.concatenate(
                [jnp.where(block == b, rv, 0.0).astype(BF16) for b in range(width // 128)], axis=1
            )
            chosen = jnp.dot(pick, wide, preferred_element_type=F32)
            high = lv.astype(BF16)
            rest = lv - high.astype(F32)
            middle = rest.astype(BF16)
            low = (rest - middle.astype(F32)).astype(BF16)
            for k in range(2):
                operand = jnp.where(which == k, chosen, 0.0).astype(BF16)
                for piece in (low, middle, high):
                    term = jnp.dot(piece, operand, preferred_element_type=F32)
                    total[k] = term if total[k] is None else total[k] + term
        for k in range(2):
            est[k] = total[k] * (1.0 / (noise_scale * 64))
        store.append(local_copy(est, est_hbm, load.at[15]))

    weight_start(0, wr_hbm, wr)
    remote(b_hbm, bv, swap_s.at[3, 0], swap_r.at[3, 0], partner, mover)
    remote(
        a_hbm.at[:, twin_half], av.at[pl.ds(0, 16)],
        swap_s.at[3, 1], swap_r.at[3, 1], twin, stays,
    )
    estimate_one()
    for k in range(CHUNKS):
        remote(
            x_hbm.at[chunk(k)], xg.at[chunk(k), mine],
            swap_s.at[0, k], swap_r.at[0, k], partner, mover,
        )
    for k in range(CHUNKS):
        remote(
            ro_hbm.at[chunk(k)], ro.at[chunk(k)],
            swap_s.at[1, k], swap_r.at[1, k], partner, mover,
        )
    x_ready(0)
    weight_relay(0, wr, 1)
    estimate_two()
    x_ready(1)
    weight_relay(0, wr, 2)
    relay(xg, 0, xy_s, xy_r)
    estimate_three()
    x_ready(2)
    weight_relay(0, wr, 3)
    relay(xg, 1, xy_s, xy_r)
    estimate_sum()
    weight_relay(0, wr, 4)
    x_ready(3)
    weight_relay(0, wr, 5)
    relay(xg, 2, xy_s, xy_r)
    weight_start(1, wo_hbm, wo)
    relay(xg, 3, xy_s, xy_r)
    pl.when(stays)(lambda: (load_a.wait(), load_b.wait(), None)[2])

    @pl.when(mover)
    def _():
        arrived(av.at[pl.ds(0, 16)], swap_r.at[3, 1])
        arrived(bv, swap_r.at[3, 0])

    weight_done(0, wr, load_wr)
    first(0)
    weight_relay(1, wo, 1)
    first(1)
    weight_relay(1, wo, 2)
    relay(gg, 0, gy_s, gy_r)
    first(2)
    weight_relay(1, wo, 3)
    relay(gg, 1, gy_s, gy_r)
    first(3)
    weight_relay(1, wo, 4)
    relay(gg, 2, gy_s, gy_r)
    weight_relay(1, wo, 5)
    weight_done(1, wo, load_wo)
    second(0)
    relay(gg, 3, gy_s, gy_r)
    for k in range(1, CHUNKS):
        second(k)

    for copy in store[:1]:
        copy.wait()

    @pl.when(stays)
    def _():
        for copy in store[1:]:
            copy.wait()

    @pl.when(mover)
    def _():
        for k in range(CHUNKS):
            arrived(out_hbm.at[chunk(k)], swap_r.at[2, k])

    for when, copy in pending:
        if when is None:
            copy.wait_send()
        else:
            pl.when(when)(copy.wait_send)


def local(inputs, readout, recept_weight, output_weight, left_vectors, right_vectors, fitness):
    members, seq_len, width = inputs.shape
    full = left_vectors.shape[2]
    rows, half = members * seq_len, full // 2
    step = rows // CHUNKS
    left = left_vectors.reshape(4, full)
    right = right_vectors.reshape(4, width)
    a = jnp.pad(left, ((0, 12), (0, 0)))
    b = jnp.pad(right, ((0, 12), (0, 0)))
    weighted = left_vectors.astype(F32) * fitness[None, :, None]
    weighted = weighted.reshape(4, 16, 2, 128).transpose(1, 2, 0, 3).reshape(16, 8, 128)
    right_tile = right_vectors.reshape(16, 128)
    anywhere = pl.BlockSpec(memory_space=pl.ANY)
    dma = pltpu.SemaphoreType.DMA
    outputs, estimate = pl.pallas_call(
        kernel,
        name="es_step",
        out_shape=(
            jax.ShapeDtypeStruct((rows, width), BF16),
            jax.ShapeDtypeStruct((2, 128, width), F32),
        ),
        in_specs=[anywhere] * 8,
        out_specs=(anywhere, anywhere),
        scratch_shapes=[
            pltpu.VMEM((rows, half), BF16),
            pltpu.VMEM((rows, half), BF16),
            pltpu.VMEM((rows, width), BF16),
            pltpu.VMEM((2, half, width), BF16),
            pltpu.VMEM((2, half, width), BF16),
            pltpu.VMEM((128, half), BF16),
            pltpu.VMEM((16, width), BF16),
            pltpu.VMEM((2 * CHUNKS, step, width + 128), F32),
            pltpu.VMEM((2 * CHUNKS, step, width + 128), F32),
            pltpu.VMEM((rows, width), BF16),
            pltpu.VMEM((4, 4, 8, 128), F32),
            pltpu.VMEM((4, 16, 128), BF16),
            pltpu.VMEM((4, 4, 8, 128), F32),
            pltpu.VMEM((4, 4, 16, 128), BF16),
            pltpu.VMEM((4, 4, 8, 128), F32),
            pltpu.VMEM((4, 4, 16, 128), BF16),
            pltpu.VMEM((2, 128, width), F32),
            dma((CHUNKS, 4)), dma((CHUNKS, 4)), dma((CHUNKS, 4)), dma((CHUNKS, 4)),
            dma((4, CHUNKS)), dma((4, CHUNKS)),
            dma((2, 2, SUBS, 2)), dma((2, 2, SUBS)),
            dma((2, 2, SUBS, 3)), dma((2, 2, SUBS, 3)),
            dma((16,)),
            dma((2 * CHUNKS,)), dma((2 * CHUNKS,)),
            dma((2, 3)), dma((2, 3)), dma((2, 3)), dma((2, 3)),
            dma((2,)), dma((2,)),
        ],
        compiler_params=pltpu.CompilerParams(
            collective_id=0, has_side_effects=True, vmem_limit_bytes=56 * 1024 * 1024
        ),
    )(
        inputs.reshape(rows, width), readout.reshape(rows, width),
        recept_weight, output_weight, a, b, weighted, right_tile,
    )
    return outputs.reshape(members, seq_len, width), estimate


def solution(mesh):
    return jax.shard_map(
        local,
        mesh=mesh,
        in_specs=(
            P("pop", None, "tensor"),
            P("pop", None, "tensor"),
            P(None, "tensor"),
            P(None, "tensor"),
            P(None, "pop", None),
            P(None, "pop", "tensor"),
            P("pop"),
        ),
        out_specs=(P("pop", None, "tensor"), P(None, "pop", "tensor")),
        check_vma=False,
    )
```

```python
import jax
import jax.numpy as jnp
from jax import lax
from jax.experimental import pallas as pl
from jax.experimental.pallas import tpu as pltpu
from jax.sharding import PartitionSpec as P

MESH = pl.DeviceIdType.MESH
noise_scale = 0.02
CHUNKS = 4
SUBS = 4
F32 = jnp.float32
BF16 = jnp.bfloat16


def mod(value, size):
    return lax.rem(value + size, size)


def device(x, y, z, core):
    return ((x * 4 + lax.rem(z, 4)) * 2 + core, (z // 4) * 4 + y)


def kernel(
    x_hbm, ro_hbm, wr_hbm, wo_hbm, left_hbm, right_hbm, fit,
    out_hbm, est_hbm,
    xg, gg, ro, wt, av, bv, proj, part_out, part_in, keep, outs,
    lv, rv, a_own, b_own, l_own, r_own, l1, r1, l2, r2, l3, r3, est,
    xy_s, xy_r, gy_s, gy_r, swap_s, swap_r, wz_s, wz_r, wx_s, wx_r,
    load, part_s, part_r, e1_s, e1_r, e2_s, e2_r, e3_s, e3_r,
):
    pop, tensor = lax.axis_index("pop"), lax.axis_index("tensor")
    x, zl, core = pop // 8, lax.rem(pop // 2, 4), lax.rem(pop, 2)
    zh, y = tensor // 4, lax.rem(tensor, 4)
    z = zh * 4 + zl
    rows, width = ro.shape
    half = xg.shape[1]
    halfquarter = half // 8
    step = rows // CHUNKS
    mover = core != zh
    stays = core == zh

    up, down = device(x, mod(y + 1, 4), z, core), device(x, mod(y + 3, 4), z, core)
    partner = device(x, y, mod(z + 4, 8), 1 - core)
    twin = device(x, y, z, 1 - core)
    z_next = (device(x, y, mod(z + 7, 8), core), device(x, y, mod(z + 1, 8), core))
    x_peer = [device(mod(x + d, 4), y, z, core) for d in range(1, 4)]
    x_up, x_down = x_peer[0], x_peer[2]
    zl_peer = [device(x, y, zh * 4 + mod(zl + d, 4), core) for d in range(1, 4)]
    z_near = [device(x, y, mod(z + d, 8), core) for d in (1, 2, 3, 5, 6, 7)]

    pending = []

    def remote(src, dst, send, recv, target, when=None):
        copy = pltpu.make_async_remote_copy(
            src_ref=src, dst_ref=dst, send_sem=send, recv_sem=recv,
            device_id=target, device_id_type=MESH,
        )
        pending.append((when, copy))
        if when is None:
            copy.start()
        else:
            pl.when(when)(copy.start)

    def arrived(dst, recv):
        pltpu.make_async_remote_copy(
            src_ref=dst, dst_ref=dst, send_sem=recv, recv_sem=recv,
            device_id=twin, device_id_type=MESH,
        ).wait_recv()

    def chunk(k, part=None):
        if part is None:
            return pl.ds(k * step, step)
        return pl.ds(k * step + part * (step // 2), step // 2)

    def columns(which):
        return pl.ds(pl.multiple_of(which * width, width), width)

    mine = columns(y)
    below, above, far = columns(mod(y + 3, 4)), columns(mod(y + 1, 4)), columns(mod(y + 2, 4))
    my_half = pl.ds(pl.multiple_of(core * half, half), half)
    twin_half = pl.ds(pl.multiple_of((1 - core) * half, half), half)

    local = []

    def local_copy(src, dst, sem, when=None):
        copy = pltpu.make_async_copy(src, dst, sem)
        if when is None:
            copy.start()
        else:
            pl.when(when)(copy.start)
        return copy

    load_left = local_copy(left_hbm, lv, load.at[1])
    load_right = local_copy(right_hbm, rv, load.at[2])
    load_x = [
        local_copy(x_hbm.at[chunk(k)], xg.at[chunk(k), mine], load.at[16 + k], stays)
        for k in range(CHUNKS)
    ]
    load_wr = local_copy(wr_hbm.at[my_half], wt.at[zh], load.at[0])
    load_ro = local_copy(ro_hbm, ro, load.at[8], stays)
    load_wo = local_copy(wo_hbm.at[my_half], wt.at[2 + zh], load.at[3])

    barrier = pltpu.get_barrier_semaphore()
    peers = [up, down, partner, twin] + x_peer + z_near
    for peer in peers:
        pl.semaphore_signal(barrier, inc=1, device_id=peer, device_id_type=MESH)

    load_left.wait()
    load_right.wait()
    left = [lv[k].astype(F32) for k in range(2)]
    right = jnp.concatenate([rv[k].astype(F32) for k in range(2)], axis=0)
    full = 2 * half
    for h in range(2):
        cut = [part[:, h * half:(h + 1) * half] for part in left]
        a_own[h] = jnp.concatenate(cut + [jnp.zeros((12, half), F32)], axis=0).astype(BF16)
    b_own[...] = jnp.concatenate([right, jnp.zeros((12, width), F32)], axis=0).astype(BF16)
    r_own[...] = jnp.concatenate(
        [right[:, b * 128:(b + 1) * 128] for b in range(width // 128)], axis=0
    ).astype(BF16)
    member = lax.broadcasted_iota(jnp.int32, (2, full), 0)
    weights = jnp.where(member == 0, fit[0], fit[1])
    weighted = jnp.concatenate([part * weights for part in left], axis=0)
    for q in range(16):
        l_own[q] = jnp.concatenate(
            [weighted[:, (2 * q + c) * 128:(2 * q + c + 1) * 128] for c in range(2)], axis=0
        )
    av[16:, :] = jnp.zeros((av.shape[0] - 16, half), BF16)

    @pl.when(stays)
    def _():
        av[:16, :] = a_own[core]
        bv[...] = b_own[...]

    l1[0] = l_own[pl.ds(4 * x, 4)]
    r1[0] = r_own[...]
    pl.semaphore_wait(barrier, len(peers))

    quarter = half // 4
    sub = quarter // SUBS
    edge = (zl == 0) | (zl == 3)
    inner = (zl == 1) | (zl == 2)
    lag = jnp.where(edge, 0, 1)
    outward = jnp.where(zl == 3, 1, 7)
    z_cross = device(x, y, mod(z + outward, 8), core)
    z_inward = device(x, y, mod(z + 8 - outward, 8), core)

    def piece(n, owner, base=0):
        start = base + owner * quarter + lax.rem(n, SUBS) * sub
        return pl.ds(pl.multiple_of(start, sub), sub)

    def held(n, owner, side):
        return wt.at[(n // SUBS) * 2 + side, piece(n, owner)]

    def weight_start(n):
        remote(
            (wr_hbm, wo_hbm)[n // SUBS].at[piece(n, x, core * half)], held(n, x, zh),
            wz_s.at[n, 0], wz_r.at[n], z_cross, edge,
        )

    def weight_send(place, n, which, target):
        return pltpu.make_async_remote_copy(
            src_ref=place, dst_ref=place, send_sem=wx_s.at[n, which],
            recv_sem=wx_r.at[n, which], device_id=target, device_id_type=MESH,
        )

    def weight_inward(place, n):
        return pltpu.make_async_remote_copy(
            src_ref=place, dst_ref=place, send_sem=wz_s.at[n, 1],
            recv_sem=wz_r.at[n], device_id=z_inward, device_id_type=MESH,
        )

    def weight_slot(slot):
        n = slot - lag

        @pl.when((n >= 0) & (n < 2 * SUBS))
        def _():
            place = held(n, x, 1 - zh)
            arrived(place, wz_r.at[n])
            pl.when(edge)(weight_inward(place, n).start)
            weight_send(place, n, 0, x_up).start()
            weight_send(place, n, 1, x_down).start()

        m = n - 1

        @pl.when((m >= 0) & (m < 2 * SUBS))
        def _():
            odd = lax.rem(m, 2)
            place = held(m, mod(x + 3 - 2 * odd, 4), 1 - zh)
            arrived(place, wx_r.at[m, odd])
            weight_send(place, m, 2, device(mod(x + 1 + 2 * odd, 4), y, z, core)).start()

    def weight_done(w):
        for n in range(w * SUBS, (w + 1) * SUBS):
            odd = n % 2
            arrived(held(n, mod(x + 1 + 2 * odd, 4), 1 - zh), wx_r.at[n, 1 - odd])
            arrived(held(n, mod(x + 2, 4), 1 - zh), wx_r.at[n, 2])

    def weight_sent():
        for n in range(2 * SUBS):
            place = held(n, x, 1 - zh)
            pl.when(edge)(weight_inward(place, n).wait_send)
            for which in range(3):
                weight_send(place, n, which, x_up).wait_send()

    def spread(buf, k, send, recv, when=None):
        place = buf.at[chunk(k), mine]
        remote(place, place, send.at[k, 0], recv.at[k, 0], up, when)
        remote(place, place, send.at[k, 1], recv.at[k, 1], down, when)

    def relay(buf, k, send, recv, when=None):
        def ready(place, sem):
            if when is None:
                arrived(place, sem)
            else:
                pl.when(when)(lambda: arrived(place, sem))

        ready(buf.at[chunk(k), below], recv.at[k, 0])
        place = buf.at[chunk(k, 0), below]
        remote(place, place, send.at[k, 2], recv.at[k, 2], up, when)
        ready(buf.at[chunk(k), above], recv.at[k, 1])
        place = buf.at[chunk(k, 1), above]
        remote(place, place, send.at[k, 3], recv.at[k, 3], down, when)

    def gathered(buf, k, recv):
        arrived(buf.at[chunk(k, 0), far], recv.at[k, 2])
        arrived(buf.at[chunk(k, 1), far], recv.at[k, 3])

    def x_ready(k, when):
        if when is stays:
            pl.when(stays)(load_x[k].wait)
        else:
            pl.when(mover)(lambda: arrived(xg.at[chunk(k), mine], swap_r.at[0, k]))
        spread(xg, k, xy_s, xy_r, when)

    def part(which, buf, k, side, sender, fresh):
        slot = which * CHUNKS + k
        value = buf[chunk(k), :]
        product = jnp.dot(value, wt[2 * which + side], preferred_element_type=F32)
        if fresh:
            proj[which, chunk(k), :] = lax.dot_general(
                value, av[...], (((1,), (1,)), ((), ())), preferred_element_type=F32
            )
        send = pltpu.make_async_remote_copy(
            src_ref=part_out.at[slot], dst_ref=part_in.at[slot],
            send_sem=part_s.at[slot], recv_sem=part_r.at[slot],
            device_id=twin, device_id_type=MESH,
        )
        pending.append((sender, send))

        @pl.when(sender)
        def _():
            part_out[slot, :, :width] = product
            part_out[slot, :, width:] = proj[which, chunk(k), :]
            send.start()

        @pl.when(jnp.logical_not(sender))
        def _():
            keep[slot] = product

    def total(which, k):
        at = which * 2 + k // (CHUNKS // 2)
        slot = which * CHUNKS + k
        arrived(part_in.at[slot], part_r.at[slot])
        scaled = noise_scale * (proj[which, chunk(k), :] + part_in[slot, :, width:])
        return (
            keep[slot] + part_in[slot, :, :width]
            + scaled[:, at:at + 1] * bv[at:at + 1, :].astype(F32)
        )

    def gate(k):
        gated = jax.nn.sigmoid(total(0, k)) * ro[chunk(k), :].astype(F32)
        gg[chunk(k), mine] = gated.astype(BF16)

    def a_part(k):
        gathered(xg, k, xy_r)
        if k == 0:
            load_wr.wait()
        part(0, xg, k, zh, mover, True)

    def a_finish(k):
        @pl.when(stays)
        def _():
            if k == 0:
                load_ro.wait()
            gate(k)

        spread(gg, k, gy_s, gy_r, stays)

    def b_part(k):
        part(0, xg, k, 1 - zh, stays, False)

    def b_finish(k):
        @pl.when(mover)
        def _():
            arrived(ro.at[chunk(k)], swap_r.at[1, k])
            gate(k)

        spread(gg, k, gy_s, gy_r, mover)

    store = []

    def c_part(k):
        gathered(gg, k, gy_r)
        part(1, gg, k, 1 - zh, stays, True)

    def c_finish(k):
        @pl.when(mover)
        def _():
            outs[chunk(k), :] = total(1, k).astype(BF16)

        remote(
            outs.at[chunk(k)], out_hbm.at[chunk(k)],
            swap_s.at[2, k], swap_r.at[2, k], partner, mover,
        )

    def d_part(k):
        part(1, gg, k, zh, mover, False)

    def d_finish(k):
        @pl.when(stays)
        def _():
            outs[chunk(k), :] = total(1, k).astype(BF16)

        store.append(local_copy(outs.at[chunk(k)], out_hbm.at[chunk(k)], load.at[16 + CHUNKS + k], stays))

    def estimate_one():
        for d in range(3):
            remote(
                l_own.at[pl.ds(4 * mod(x + d + 1, 4), 4)], l1.at[d + 1],
                e1_s.at[0, d], e1_r.at[0, d], x_peer[d],
            )
            remote(r_own, r1.at[d + 1], e1_s.at[1, d], e1_r.at[1, d], x_peer[d])

    def estimate_two():
        for d in range(3):
            arrived(l1.at[d + 1], e1_r.at[0, d])
            arrived(r1.at[d + 1], e1_r.at[1, d])
        for d in range(3):
            remote(
                l1.at[:, mod(zl + d + 1, 4)], l2.at[d + 1],
                e2_s.at[0, d], e2_r.at[0, d], zl_peer[d],
            )
            remote(r1, r2.at[d + 1], e2_s.at[1, d], e2_r.at[1, d], zl_peer[d])
        l2[0] = l1[:, zl]
        r2[0] = r1[...]

    def estimate_three():
        for d in range(3):
            arrived(l2.at[d + 1], e2_r.at[0, d])
            arrived(r2.at[d + 1], e2_r.at[1, d])
        remote(l2, l3, e3_s.at[0], e3_r.at[0], twin)
        remote(r2, r3, e3_s.at[1], e3_r.at[1], twin)

    def estimate_sum():
        arrived(l3, e3_r.at[0])
        arrived(r3, e3_r.at[1])
        n = 16
        lrow = lax.broadcasted_iota(jnp.int32, (n * 8, n * 16), 0)
        rrow = lax.broadcasted_iota(jnp.int32, (n * 8, n * 16), 1)
        same = (lrow // 8 == rrow // 16) & (lrow % 8 == core * 4 + rrow % 4)
        pick = jnp.where(same, 1.0, 0.0).astype(BF16)
        block = (lax.broadcasted_iota(jnp.int32, (n * 16, 128), 0) % 16) // 4
        which = (lax.broadcasted_iota(jnp.int32, (n * 8, width), 0) // 2) % 2
        sums = [None, None]
        for left, right in ((l2, r2), (l3, r3)):
            lt = left[...].reshape(n * 8, 128).T
            rt = right[...].reshape(n * 16, 128).astype(F32)
            wide = jnp.concatenate(
                [jnp.where(block == b, rt, 0.0).astype(BF16) for b in range(width // 128)], axis=1
            )
            chosen = jnp.dot(pick, wide, preferred_element_type=F32)
            high = lt.astype(BF16)
            rest = lt - high.astype(F32)
            middle = rest.astype(BF16)
            low = (rest - middle.astype(F32)).astype(BF16)
            for k in range(2):
                operand = jnp.where(which == k, chosen, 0.0).astype(BF16)
                for piece in (low, middle, high):
                    term = jnp.dot(piece, operand, preferred_element_type=F32)
                    sums[k] = term if sums[k] is None else sums[k] + term
        for k in range(2):
            est[k] = sums[k]
        store.append(local_copy(est, est_hbm, load.at[15]))

    def x_swap(k):
        remote(
            x_hbm.at[chunk(k)], xg.at[chunk(k), mine],
            swap_s.at[0, k], swap_r.at[0, k], partner, mover,
        )

    def ro_swap(k):
        remote(
            ro_hbm.at[chunk(k)], ro.at[chunk(k)],
            swap_s.at[1, k], swap_r.at[1, k], partner, mover,
        )

    def x_relay(k, when):
        relay(xg, k, xy_s, xy_r, when)

    def g_relay(k, when):
        relay(gg, k, gy_s, gy_r, when)

    x_ready(0, stays)
    weight_start(0)
    weight_start(1)
    x_swap(0)
    weight_start(2)
    x_relay(0, stays)
    x_ready(1, stays)

    remote(b_own, bv, swap_s.at[3, 0], swap_r.at[3, 0], partner, mover)
    remote(
        a_own.at[1 - core], av.at[pl.ds(0, 16)],
        swap_s.at[3, 1], swap_r.at[3, 1], twin, stays,
    )
    estimate_one()
    weight_slot(0)
    weight_start(3)
    weight_start(4)
    x_ready(2, stays)
    x_relay(1, stays)
    x_swap(1)
    x_ready(0, mover)
    x_ready(3, stays)
    weight_slot(1)
    x_relay(0, mover)
    weight_start(5)
    x_swap(2)
    weight_start(6)
    x_ready(1, mover)
    weight_slot(2)

    @pl.when(mover)
    def _():
        arrived(av.at[pl.ds(0, 16)], swap_r.at[3, 1])
        arrived(bv, swap_r.at[3, 0])

    a_part(0)
    x_swap(3)
    x_relay(1, mover)
    ro_swap(0)
    estimate_two()
    weight_slot(3)
    x_ready(2, mover)
    a_part(1)
    x_relay(2, stays)
    weight_slot(4)
    ro_swap(1)
    a_finish(0)
    weight_start(7)
    x_relay(2, mover)
    weight_slot(5)
    x_ready(3, mover)
    a_part(2)
    x_relay(3, stays)
    weight_done(0)
    b_part(0)
    estimate_three()
    weight_slot(6)
    x_relay(3, mover)
    b_finish(0)
    a_part(3)
    g_relay(0, stays)
    a_finish(1)
    a_finish(2)
    weight_slot(7)
    b_part(1)
    b_part(2)
    ro_swap(2)
    g_relay(0, mover)
    b_part(3)
    weight_slot(8)
    b_finish(1)
    g_relay(1, stays)
    a_finish(3)
    g_relay(2, stays)
    weight_slot(9)
    ro_swap(3)
    b_finish(2)
    load_wo.wait()
    weight_done(1)
    estimate_sum()
    c_part(0)
    g_relay(1, mover)
    c_finish(0)
    d_part(0)
    g_relay(2, mover)
    b_finish(3)
    c_part(1)
    g_relay(3, stays)
    c_finish(1)
    c_part(2)
    d_part(1)
    g_relay(3, mover)
    d_finish(0)
    c_finish(2)
    d_part(2)
    c_part(3)
    d_finish(1)
    d_finish(2)
    d_part(3)
    c_finish(3)
    d_finish(3)

    for copy in store[:1]:
        copy.wait()

    @pl.when(stays)
    def _():
        for copy in store[1:]:
            copy.wait()

    @pl.when(mover)
    def _():
        for k in range(CHUNKS):
            arrived(out_hbm.at[chunk(k)], swap_r.at[2, k])

    weight_sent()
    for when, copy in pending:
        if when is None:
            copy.wait_send()
        else:
            pl.when(when)(copy.wait_send)


def local(inputs, readout, recept_weight, output_weight, left_vectors, right_vectors, fitness):
    members, seq_len, width = inputs.shape
    full = left_vectors.shape[2]
    rows, half = members * seq_len, full // 2
    step = rows // CHUNKS
    anywhere = pl.BlockSpec(memory_space=pl.ANY)
    dma = pltpu.SemaphoreType.DMA
    outputs, estimate = pl.pallas_call(
        kernel,
        name="es_step",
        out_shape=(
            jax.ShapeDtypeStruct((rows, width), BF16),
            jax.ShapeDtypeStruct((2, 128, width), F32),
        ),
        in_specs=[anywhere] * 6 + [pl.BlockSpec(memory_space=pltpu.SMEM)],
        out_specs=(anywhere, anywhere),
        scratch_shapes=[
            pltpu.VMEM((rows, half), BF16),
            pltpu.VMEM((rows, half), BF16),
            pltpu.VMEM((rows, width), BF16),
            pltpu.VMEM((4, half, width), BF16),
            pltpu.VMEM((128, half), BF16),
            pltpu.VMEM((16, width), BF16),
            pltpu.VMEM((2, rows, 128), F32),
            pltpu.VMEM((2 * CHUNKS, step, width + 128), F32),
            pltpu.VMEM((2 * CHUNKS, step, width + 128), F32),
            pltpu.VMEM((2 * CHUNKS, step, width), F32),
            pltpu.VMEM((rows, width), BF16),
            pltpu.VMEM((2, members, full), BF16),
            pltpu.VMEM((2, members, width), BF16),
            pltpu.VMEM((2, 16, half), BF16),
            pltpu.VMEM((16, width), BF16),
            pltpu.VMEM((16, 8, 128), F32),
            pltpu.VMEM((16, 128), BF16),
            pltpu.VMEM((4, 4, 8, 128), F32),
            pltpu.VMEM((4, 16, 128), BF16),
            pltpu.VMEM((4, 4, 8, 128), F32),
            pltpu.VMEM((4, 4, 16, 128), BF16),
            pltpu.VMEM((4, 4, 8, 128), F32),
            pltpu.VMEM((4, 4, 16, 128), BF16),
            pltpu.VMEM((2, 128, width), F32),
            dma((CHUNKS, 4)), dma((CHUNKS, 4)), dma((CHUNKS, 4)), dma((CHUNKS, 4)),
            dma((4, CHUNKS)), dma((4, CHUNKS)),
            dma((2 * SUBS, 2)), dma((2 * SUBS,)),
            dma((2 * SUBS, 3)), dma((2 * SUBS, 3)),
            dma((16 + 2 * CHUNKS,)),
            dma((2 * CHUNKS,)), dma((2 * CHUNKS,)),
            dma((2, 3)), dma((2, 3)), dma((2, 3)), dma((2, 3)),
            dma((2,)), dma((2,)),
        ],
        compiler_params=pltpu.CompilerParams(
            collective_id=0, has_side_effects=True, vmem_limit_bytes=56 * 1024 * 1024
        ),
    )(
        inputs.reshape(rows, width), readout.reshape(rows, width),
        recept_weight, output_weight, left_vectors, right_vectors, fitness,
    )
    return outputs.reshape(members, seq_len, width), estimate * (1.0 / (noise_scale * 64))


def solution(mesh):
    return jax.shard_map(
        local,
        mesh=mesh,
        in_specs=(
            P("pop", None, "tensor"),
            P("pop", None, "tensor"),
            P(None, "tensor"),
            P(None, "tensor"),
            P(None, "pop", None),
            P(None, "pop", "tensor"),
            P("pop"),
        ),
        out_specs=(P("pop", None, "tensor"), P(None, "pop", "tensor")),
        check_vma=False,
    )
```

```python
import jax
import jax.numpy as jnp
from jax import lax
from jax.experimental import pallas as pl
from jax.experimental.pallas import tpu as pltpu
from jax.sharding import PartitionSpec as P

MESH = pl.DeviceIdType.MESH
noise_scale = 0.02
CHUNKS = 4
SUBS = 4
F32 = jnp.float32
BF16 = jnp.bfloat16


def mod(value, size):
    return lax.rem(value + size, size)


def device(x, y, z, core):
    return ((x * 4 + lax.rem(z, 4)) * 2 + core, (z // 4) * 4 + y)


def kernel(
    x_hbm, ro_hbm, wr_hbm, wo_hbm, left_hbm, right_hbm, fit,
    out_hbm, est_hbm,
    xg, gg, ro, wt, av, bv, proj, part_out, part_in, keep, outs,
    lv, rv, a_own, b_own, l_own, r_own, l1, r1, l2, r2, l3, r3, est,
    xy_s, xy_r, gy_s, gy_r, swap_s, swap_r, wz_s, wz_r, wx_s, wx_r,
    load, part_s, part_r, e1_s, e1_r, e2_s, e2_r, e3_s, e3_r,
):
    pop, tensor = lax.axis_index("pop"), lax.axis_index("tensor")
    x, zl, core = pop // 8, lax.rem(pop // 2, 4), lax.rem(pop, 2)
    zh, y = tensor // 4, lax.rem(tensor, 4)
    z = zh * 4 + zl
    rows, width = ro.shape
    half = xg.shape[1]
    halfquarter = half // 8
    step = rows // CHUNKS
    mover = core != zh
    stays = core == zh

    up, down = device(x, mod(y + 1, 4), z, core), device(x, mod(y + 3, 4), z, core)
    partner = device(x, y, mod(z + 4, 8), 1 - core)
    twin = device(x, y, z, 1 - core)
    z_next = (device(x, y, mod(z + 7, 8), core), device(x, y, mod(z + 1, 8), core))
    x_peer = [device(mod(x + d, 4), y, z, core) for d in range(1, 4)]
    x_up, x_down = x_peer[0], x_peer[2]
    zl_peer = [device(x, y, zh * 4 + mod(zl + d, 4), core) for d in range(1, 4)]
    z_near = [device(x, y, mod(z + d, 8), core) for d in (1, 2, 3, 5, 6, 7)]

    pending = []

    def remote(src, dst, send, recv, target, when=None):
        copy = pltpu.make_async_remote_copy(
            src_ref=src, dst_ref=dst, send_sem=send, recv_sem=recv,
            device_id=target, device_id_type=MESH,
        )
        pending.append((when, copy))
        if when is None:
            copy.start()
        else:
            pl.when(when)(copy.start)

    def arrived(dst, recv):
        pltpu.make_async_remote_copy(
            src_ref=dst, dst_ref=dst, send_sem=recv, recv_sem=recv,
            device_id=twin, device_id_type=MESH,
        ).wait_recv()

    def chunk(k, part=None):
        if part is None:
            return pl.ds(k * step, step)
        return pl.ds(k * step + part * (step // 2), step // 2)

    def columns(which):
        return pl.ds(pl.multiple_of(which * width, width), width)

    mine = columns(y)
    below, above, far = columns(mod(y + 3, 4)), columns(mod(y + 1, 4)), columns(mod(y + 2, 4))
    my_half = pl.ds(pl.multiple_of(core * half, half), half)
    twin_half = pl.ds(pl.multiple_of((1 - core) * half, half), half)

    local = []

    def local_copy(src, dst, sem, when=None):
        copy = pltpu.make_async_copy(src, dst, sem)
        if when is None:
            copy.start()
        else:
            pl.when(when)(copy.start)
        return copy

    load_left = local_copy(left_hbm, lv, load.at[1])
    load_right = local_copy(right_hbm, rv, load.at[2])
    load_x = [
        local_copy(x_hbm.at[chunk(k)], xg.at[chunk(k), mine], load.at[16 + k], stays)
        for k in range(CHUNKS)
    ]
    load_wr = local_copy(wr_hbm.at[my_half], wt.at[zh], load.at[0])
    load_ro = local_copy(ro_hbm, ro, load.at[8], stays)
    load_wo = local_copy(wo_hbm.at[my_half], wt.at[2 + zh], load.at[3])

    barrier = pltpu.get_barrier_semaphore()
    peers = [up, down, partner, twin] + x_peer + z_near
    for peer in peers:
        pl.semaphore_signal(barrier, inc=1, device_id=peer, device_id_type=MESH)

    load_left.wait()
    load_right.wait()
    left = [lv[k].astype(F32) for k in range(2)]
    right = jnp.concatenate([rv[k].astype(F32) for k in range(2)], axis=0)
    full = 2 * half
    for h in range(2):
        cut = [part[:, h * half:(h + 1) * half] for part in left]
        a_own[h] = jnp.concatenate(cut + [jnp.zeros((12, half), F32)], axis=0).astype(BF16)
    b_own[...] = jnp.concatenate([right, jnp.zeros((12, width), F32)], axis=0).astype(BF16)
    r_own[...] = jnp.concatenate(
        [right[:, b * 128:(b + 1) * 128] for b in range(width // 128)], axis=0
    ).astype(BF16)
    member = lax.broadcasted_iota(jnp.int32, (2, full), 0)
    weights = jnp.where(member == 0, fit[0], fit[1])
    weighted = jnp.concatenate([part * weights for part in left], axis=0)
    for q in range(16):
        l_own[q] = jnp.concatenate(
            [weighted[:, (2 * q + c) * 128:(2 * q + c + 1) * 128] for c in range(2)], axis=0
        )
    av[16:, :] = jnp.zeros((av.shape[0] - 16, half), BF16)

    @pl.when(stays)
    def _():
        av[:16, :] = a_own[core]
        bv[...] = b_own[...]

    l1[0] = l_own[pl.ds(4 * x, 4)]
    r1[0] = r_own[...]
    pl.semaphore_wait(barrier, len(peers))

    quarter = half // 4
    sub = quarter // SUBS
    edge = (zl == 0) | (zl == 3)
    inner = (zl == 1) | (zl == 2)
    lag = jnp.where(edge, 0, 1)
    outward = jnp.where(zl == 3, 1, 7)
    z_cross = device(x, y, mod(z + outward, 8), core)
    z_inward = device(x, y, mod(z + 8 - outward, 8), core)

    def piece(n, owner, base=0):
        start = base + owner * quarter + lax.rem(n, SUBS) * sub
        return pl.ds(pl.multiple_of(start, sub), sub)

    def held(n, owner, side):
        return wt.at[(n // SUBS) * 2 + side, piece(n, owner)]

    def weight_start(n):
        remote(
            (wr_hbm, wo_hbm)[n // SUBS].at[piece(n, x, core * half)], held(n, x, zh),
            wz_s.at[n, 0], wz_r.at[n], z_cross, edge,
        )

    def weight_send(place, n, which, target):
        return pltpu.make_async_remote_copy(
            src_ref=place, dst_ref=place, send_sem=wx_s.at[n, which],
            recv_sem=wx_r.at[n, which], device_id=target, device_id_type=MESH,
        )

    def weight_inward(place, n):
        return pltpu.make_async_remote_copy(
            src_ref=place, dst_ref=place, send_sem=wz_s.at[n, 1],
            recv_sem=wz_r.at[n], device_id=z_inward, device_id_type=MESH,
        )

    def weight_slot(slot):
        n = slot - lag

        @pl.when((n >= 0) & (n < 2 * SUBS))
        def _():
            place = held(n, x, 1 - zh)
            arrived(place, wz_r.at[n])
            pl.when(edge)(weight_inward(place, n).start)
            weight_send(place, n, 0, x_up).start()
            weight_send(place, n, 1, x_down).start()

        m = n - 2

        @pl.when((m >= 0) & (m < 2 * SUBS))
        def _():
            odd = lax.rem(m, 2)
            place = held(m, mod(x + 3 - 2 * odd, 4), 1 - zh)
            arrived(place, wx_r.at[m, odd])
            weight_send(place, m, 2, device(mod(x + 1 + 2 * odd, 4), y, z, core)).start()

    def weight_done(w):
        for n in range(w * SUBS, (w + 1) * SUBS):
            odd = n % 2
            arrived(held(n, mod(x + 1 + 2 * odd, 4), 1 - zh), wx_r.at[n, 1 - odd])
            arrived(held(n, mod(x + 2, 4), 1 - zh), wx_r.at[n, 2])

    def weight_sent():
        for n in range(2 * SUBS):
            place = held(n, x, 1 - zh)
            pl.when(edge)(weight_inward(place, n).wait_send)
            for which in range(3):
                weight_send(place, n, which, x_up).wait_send()

    def spread(buf, k, send, recv, when=None):
        place = buf.at[chunk(k), mine]
        remote(place, place, send.at[k, 0], recv.at[k, 0], up, when)
        remote(place, place, send.at[k, 1], recv.at[k, 1], down, when)

    def relay(buf, k, send, recv, when=None):
        def ready(place, sem):
            if when is None:
                arrived(place, sem)
            else:
                pl.when(when)(lambda: arrived(place, sem))

        ready(buf.at[chunk(k), below], recv.at[k, 0])
        place = buf.at[chunk(k, 0), below]
        remote(place, place, send.at[k, 2], recv.at[k, 2], up, when)
        ready(buf.at[chunk(k), above], recv.at[k, 1])
        place = buf.at[chunk(k, 1), above]
        remote(place, place, send.at[k, 3], recv.at[k, 3], down, when)

    def gathered(buf, k, recv):
        arrived(buf.at[chunk(k, 0), far], recv.at[k, 2])
        arrived(buf.at[chunk(k, 1), far], recv.at[k, 3])

    def x_ready(k, when):
        if when is stays:
            pl.when(stays)(load_x[k].wait)
        else:
            pl.when(mover)(lambda: arrived(xg.at[chunk(k), mine], swap_r.at[0, k]))
        spread(xg, k, xy_s, xy_r, when)

    def part(which, buf, k, side, sender, fresh):
        slot = which * CHUNKS + k
        value = buf[chunk(k), :]
        product = jnp.dot(value, wt[2 * which + side], preferred_element_type=F32)
        if fresh:
            proj[which, chunk(k), :] = lax.dot_general(
                value, av[...], (((1,), (1,)), ((), ())), preferred_element_type=F32
            )
        send = pltpu.make_async_remote_copy(
            src_ref=part_out.at[slot], dst_ref=part_in.at[slot],
            send_sem=part_s.at[slot], recv_sem=part_r.at[slot],
            device_id=twin, device_id_type=MESH,
        )
        pending.append((sender, send))

        @pl.when(sender)
        def _():
            part_out[slot, :, :width] = product
            part_out[slot, :, width:] = proj[which, chunk(k), :]
            send.start()

        @pl.when(jnp.logical_not(sender))
        def _():
            keep[slot] = product

    def total(which, k):
        at = which * 2 + k // (CHUNKS // 2)
        slot = which * CHUNKS + k
        arrived(part_in.at[slot], part_r.at[slot])
        scaled = noise_scale * (proj[which, chunk(k), :] + part_in[slot, :, width:])
        return (
            keep[slot] + part_in[slot, :, :width]
            + scaled[:, at:at + 1] * bv[at:at + 1, :].astype(F32)
        )

    def gate(k):
        gated = jax.nn.sigmoid(total(0, k)) * ro[chunk(k), :].astype(F32)
        gg[chunk(k), mine] = gated.astype(BF16)

    def a_part(k):
        gathered(xg, k, xy_r)
        if k == 0:
            load_wr.wait()
        part(0, xg, k, zh, mover, True)

    def a_finish(k):
        @pl.when(stays)
        def _():
            if k == 0:
                load_ro.wait()
            gate(k)

        spread(gg, k, gy_s, gy_r, stays)

    def b_part(k):
        part(0, xg, k, 1 - zh, stays, False)

    def b_finish(k):
        @pl.when(mover)
        def _():
            arrived(ro.at[chunk(k)], swap_r.at[1, k])
            gate(k)

        spread(gg, k, gy_s, gy_r, mover)

    store = []

    def c_part(k):
        gathered(gg, k, gy_r)
        part(1, gg, k, 1 - zh, stays, True)

    def c_finish(k):
        @pl.when(mover)
        def _():
            outs[chunk(k), :] = total(1, k).astype(BF16)

        remote(
            outs.at[chunk(k)], out_hbm.at[chunk(k)],
            swap_s.at[2, k], swap_r.at[2, k], partner, mover,
        )

    def d_part(k):
        part(1, gg, k, zh, mover, False)

    def d_finish(k):
        @pl.when(stays)
        def _():
            outs[chunk(k), :] = total(1, k).astype(BF16)

        store.append(local_copy(outs.at[chunk(k)], out_hbm.at[chunk(k)], load.at[16 + CHUNKS + k], stays))

    def estimate_one():
        for d in range(3):
            remote(
                l_own.at[pl.ds(4 * mod(x + d + 1, 4), 4)], l1.at[d + 1],
                e1_s.at[0, d], e1_r.at[0, d], x_peer[d],
            )
            remote(r_own, r1.at[d + 1], e1_s.at[1, d], e1_r.at[1, d], x_peer[d])

    def estimate_two():
        for d in range(3):
            arrived(l1.at[d + 1], e1_r.at[0, d])
            arrived(r1.at[d + 1], e1_r.at[1, d])
        for d in range(3):
            remote(
                l1.at[:, mod(zl + d + 1, 4)], l2.at[d + 1],
                e2_s.at[0, d], e2_r.at[0, d], zl_peer[d],
            )
            remote(r1, r2.at[d + 1], e2_s.at[1, d], e2_r.at[1, d], zl_peer[d])
        l2[0] = l1[:, zl]
        r2[0] = r1[...]

    def estimate_three():
        for d in range(3):
            arrived(l2.at[d + 1], e2_r.at[0, d])
            arrived(r2.at[d + 1], e2_r.at[1, d])
        remote(l2, l3, e3_s.at[0], e3_r.at[0], twin)
        remote(r2, r3, e3_s.at[1], e3_r.at[1], twin)

    def estimate_sum():
        arrived(l3, e3_r.at[0])
        arrived(r3, e3_r.at[1])
        n = 16
        lrow = lax.broadcasted_iota(jnp.int32, (n * 8, n * 16), 0)
        rrow = lax.broadcasted_iota(jnp.int32, (n * 8, n * 16), 1)
        same = (lrow // 8 == rrow // 16) & (lrow % 8 == core * 4 + rrow % 4)
        pick = jnp.where(same, 1.0, 0.0).astype(BF16)
        block = (lax.broadcasted_iota(jnp.int32, (n * 16, 128), 0) % 16) // 4
        which = (lax.broadcasted_iota(jnp.int32, (n * 8, width), 0) // 2) % 2
        sums = [None, None]
        for left, right in ((l2, r2), (l3, r3)):
            lt = left[...].reshape(n * 8, 128).T
            rt = right[...].reshape(n * 16, 128).astype(F32)
            wide = jnp.concatenate(
                [jnp.where(block == b, rt, 0.0).astype(BF16) for b in range(width // 128)], axis=1
            )
            chosen = jnp.dot(pick, wide, preferred_element_type=F32)
            high = lt.astype(BF16)
            rest = lt - high.astype(F32)
            middle = rest.astype(BF16)
            low = (rest - middle.astype(F32)).astype(BF16)
            for k in range(2):
                operand = jnp.where(which == k, chosen, 0.0).astype(BF16)
                for piece in (low, middle, high):
                    term = jnp.dot(piece, operand, preferred_element_type=F32)
                    sums[k] = term if sums[k] is None else sums[k] + term
        for k in range(2):
            est[k] = sums[k]
        store.append(local_copy(est, est_hbm, load.at[15]))

    def x_swap(k):
        remote(
            x_hbm.at[chunk(k)], xg.at[chunk(k), mine],
            swap_s.at[0, k], swap_r.at[0, k], partner, mover,
        )

    def ro_swap(k):
        remote(
            ro_hbm.at[chunk(k)], ro.at[chunk(k)],
            swap_s.at[1, k], swap_r.at[1, k], partner, mover,
        )

    def x_relay(k, when):
        relay(xg, k, xy_s, xy_r, when)

    def g_relay(k, when):
        relay(gg, k, gy_s, gy_r, when)

    x_ready(0, stays)
    x_relay(0, stays)
    x_swap(0)
    weight_start(0)
    x_ready(1, stays)
    weight_start(1)
    x_swap(1)
    x_ready(0, mover)
    weight_start(2)
    weight_start(3)
    x_ready(2, stays)
    x_relay(1, stays)

    remote(b_own, bv, swap_s.at[3, 0], swap_r.at[3, 0], partner, mover)
    remote(
        a_own.at[1 - core], av.at[pl.ds(0, 16)],
        swap_s.at[3, 1], swap_r.at[3, 1], twin, stays,
    )
    estimate_one()
    weight_slot(0)
    x_swap(2)
    weight_start(4)
    x_relay(2, stays)
    x_ready(3, stays)
    x_relay(0, mover)
    weight_start(5)
    weight_slot(1)

    @pl.when(mover)
    def _():
        arrived(av.at[pl.ds(0, 16)], swap_r.at[3, 1])
        arrived(bv, swap_r.at[3, 0])

    a_part(0)
    weight_slot(2)
    x_ready(1, mover)
    estimate_two()
    weight_slot(3)
    weight_start(6)
    x_ready(2, mover)
    x_relay(1, mover)
    x_swap(3)
    a_finish(0)
    weight_slot(4)
    x_relay(2, mover)
    weight_slot(5)
    estimate_three()
    weight_slot(6)
    a_part(1)
    weight_start(7)
    a_finish(1)
    x_ready(3, mover)
    g_relay(0, stays)
    ro_swap(0)
    weight_done(0)
    x_relay(3, stays)
    weight_slot(7)
    x_relay(3, mover)
    b_part(0)
    g_relay(1, stays)
    ro_swap(1)
    a_part(2)
    b_part(1)
    weight_slot(8)
    a_finish(2)
    a_part(3)
    b_part(2)
    b_finish(0)
    ro_swap(2)
    ro_swap(3)
    weight_slot(9)
    b_finish(1)
    weight_slot(10)
    g_relay(0, mover)
    b_part(3)
    g_relay(1, mover)
    g_relay(2, stays)
    load_wo.wait()
    weight_done(1)
    b_finish(2)
    estimate_sum()
    c_part(0)
    c_finish(0)
    a_finish(3)
    b_finish(3)
    c_part(1)
    g_relay(3, stays)
    c_finish(1)
    d_part(0)
    g_relay(2, mover)
    g_relay(3, mover)
    d_part(1)
    c_part(2)
    d_finish(0)
    c_finish(2)
    d_part(2)
    c_part(3)
    c_finish(3)
    d_part(3)
    d_finish(1)
    d_finish(2)
    d_finish(3)

    for copy in store[:1]:
        copy.wait()

    @pl.when(stays)
    def _():
        for copy in store[1:]:
            copy.wait()

    @pl.when(mover)
    def _():
        for k in range(CHUNKS):
            arrived(out_hbm.at[chunk(k)], swap_r.at[2, k])

    weight_sent()
    for when, copy in pending:
        if when is None:
            copy.wait_send()
        else:
            pl.when(when)(copy.wait_send)


def local(inputs, readout, recept_weight, output_weight, left_vectors, right_vectors, fitness):
    members, seq_len, width = inputs.shape
    full = left_vectors.shape[2]
    rows, half = members * seq_len, full // 2
    step = rows // CHUNKS
    anywhere = pl.BlockSpec(memory_space=pl.ANY)
    dma = pltpu.SemaphoreType.DMA
    outputs, estimate = pl.pallas_call(
        kernel,
        name="es_step",
        out_shape=(
            jax.ShapeDtypeStruct((rows, width), BF16),
            jax.ShapeDtypeStruct((2, 128, width), F32),
        ),
        in_specs=[anywhere] * 6 + [pl.BlockSpec(memory_space=pltpu.SMEM)],
        out_specs=(anywhere, anywhere),
        scratch_shapes=[
            pltpu.VMEM((rows, half), BF16),
            pltpu.VMEM((rows, half), BF16),
            pltpu.VMEM((rows, width), BF16),
            pltpu.VMEM((4, half, width), BF16),
            pltpu.VMEM((128, half), BF16),
            pltpu.VMEM((16, width), BF16),
            pltpu.VMEM((2, rows, 128), F32),
            pltpu.VMEM((2 * CHUNKS, step, width + 128), F32),
            pltpu.VMEM((2 * CHUNKS, step, width + 128), F32),
            pltpu.VMEM((2 * CHUNKS, step, width), F32),
            pltpu.VMEM((rows, width), BF16),
            pltpu.VMEM((2, members, full), BF16),
            pltpu.VMEM((2, members, width), BF16),
            pltpu.VMEM((2, 16, half), BF16),
            pltpu.VMEM((16, width), BF16),
            pltpu.VMEM((16, 8, 128), F32),
            pltpu.VMEM((16, 128), BF16),
            pltpu.VMEM((4, 4, 8, 128), F32),
            pltpu.VMEM((4, 16, 128), BF16),
            pltpu.VMEM((4, 4, 8, 128), F32),
            pltpu.VMEM((4, 4, 16, 128), BF16),
            pltpu.VMEM((4, 4, 8, 128), F32),
            pltpu.VMEM((4, 4, 16, 128), BF16),
            pltpu.VMEM((2, 128, width), F32),
            dma((CHUNKS, 4)), dma((CHUNKS, 4)), dma((CHUNKS, 4)), dma((CHUNKS, 4)),
            dma((4, CHUNKS)), dma((4, CHUNKS)),
            dma((2 * SUBS, 2)), dma((2 * SUBS,)),
            dma((2 * SUBS, 3)), dma((2 * SUBS, 3)),
            dma((16 + 2 * CHUNKS,)),
            dma((2 * CHUNKS,)), dma((2 * CHUNKS,)),
            dma((2, 3)), dma((2, 3)), dma((2, 3)), dma((2, 3)),
            dma((2,)), dma((2,)),
        ],
        compiler_params=pltpu.CompilerParams(
            collective_id=0, has_side_effects=True, vmem_limit_bytes=56 * 1024 * 1024
        ),
    )(
        inputs.reshape(rows, width), readout.reshape(rows, width),
        recept_weight, output_weight, left_vectors, right_vectors, fitness,
    )
    return outputs.reshape(members, seq_len, width), estimate * (1.0 / (noise_scale * 64))


def solution(mesh):
    return jax.shard_map(
        local,
        mesh=mesh,
        in_specs=(
            P("pop", None, "tensor"),
            P("pop", None, "tensor"),
            P(None, "tensor"),
            P(None, "tensor"),
            P(None, "pop", None),
            P(None, "pop", "tensor"),
            P("pop"),
        ),
        out_specs=(P("pop", None, "tensor"), P(None, "pop", "tensor")),
        check_vma=False,
    )
```

```python
import jax
import jax.numpy as jnp
from jax import lax
from jax.experimental import pallas as pl
from jax.experimental.pallas import tpu as pltpu
from jax.sharding import PartitionSpec as P

MESH = pl.DeviceIdType.MESH
noise_scale = 0.02
CHUNKS = 4
SUBS = 4
F32 = jnp.float32
BF16 = jnp.bfloat16


def mod(value, size):
    return lax.rem(value + size, size)


def device(x, y, z, core):
    return ((x * 4 + lax.rem(z, 4)) * 2 + core, (z // 4) * 4 + y)


def kernel(
    x_hbm, ro_hbm, wr_hbm, wo_hbm, left_hbm, right_hbm, fit,
    out_hbm, est_hbm,
    xg, gg, ro, wt, av, bv, proj, part_out, part_in, keep, outs,
    lv, rv, a_own, b_own, l_own, r_own, l1, r1, l2, r2, l3, r3, est,
    xy_s, xy_r, gy_s, gy_r, swap_s, swap_r, wz_s, wz_r, wx_s, wx_r,
    load, part_s, part_r, e1_s, e1_r, e2_s, e2_r, e3_s, e3_r,
):
    pop, tensor = lax.axis_index("pop"), lax.axis_index("tensor")
    x, zl, core = pop // 8, lax.rem(pop // 2, 4), lax.rem(pop, 2)
    zh, y = tensor // 4, lax.rem(tensor, 4)
    z = zh * 4 + zl
    rows, width = ro.shape
    half = xg.shape[1]
    halfquarter = half // 8
    step = rows // CHUNKS
    mover = core != zh
    stays = core == zh

    up, down = device(x, mod(y + 1, 4), z, core), device(x, mod(y + 3, 4), z, core)
    partner = device(x, y, mod(z + 4, 8), 1 - core)
    twin = device(x, y, z, 1 - core)
    z_next = (device(x, y, mod(z + 7, 8), core), device(x, y, mod(z + 1, 8), core))
    x_peer = [device(mod(x + d, 4), y, z, core) for d in range(1, 4)]
    x_up, x_down = x_peer[0], x_peer[2]
    zl_peer = [device(x, y, zh * 4 + mod(zl + d, 4), core) for d in range(1, 4)]
    z_near = [device(x, y, mod(z + d, 8), core) for d in (1, 2, 3, 5, 6, 7)]

    pending = []

    def remote(src, dst, send, recv, target, when=None):
        copy = pltpu.make_async_remote_copy(
            src_ref=src, dst_ref=dst, send_sem=send, recv_sem=recv,
            device_id=target, device_id_type=MESH,
        )
        pending.append((when, copy))
        if when is None:
            copy.start()
        else:
            pl.when(when)(copy.start)

    def arrived(dst, recv):
        pltpu.make_async_remote_copy(
            src_ref=dst, dst_ref=dst, send_sem=recv, recv_sem=recv,
            device_id=twin, device_id_type=MESH,
        ).wait_recv()

    def chunk(k, part=None):
        if part is None:
            return pl.ds(k * step, step)
        return pl.ds(k * step + part * (step // 2), step // 2)

    def columns(which):
        return pl.ds(pl.multiple_of(which * width, width), width)

    mine = columns(y)
    below, above, far = columns(mod(y + 3, 4)), columns(mod(y + 1, 4)), columns(mod(y + 2, 4))
    my_half = pl.ds(pl.multiple_of(core * half, half), half)
    twin_half = pl.ds(pl.multiple_of((1 - core) * half, half), half)

    local = []

    def local_copy(src, dst, sem, when=None):
        copy = pltpu.make_async_copy(src, dst, sem)
        if when is None:
            copy.start()
        else:
            pl.when(when)(copy.start)
        return copy

    load_left = local_copy(left_hbm, lv, load.at[1])
    load_right = local_copy(right_hbm, rv, load.at[2])
    load_x = [
        local_copy(x_hbm.at[chunk(k)], xg.at[chunk(k), mine], load.at[16 + k], stays)
        for k in range(CHUNKS)
    ]
    load_wr = local_copy(wr_hbm.at[my_half], wt.at[zh], load.at[0])
    load_ro = local_copy(ro_hbm, ro, load.at[8], stays)
    load_wo = local_copy(wo_hbm.at[my_half], wt.at[2 + zh], load.at[3])

    barrier = pltpu.get_barrier_semaphore()
    peers = [up, down, partner, twin] + x_peer + z_near
    for peer in peers:
        pl.semaphore_signal(barrier, inc=1, device_id=peer, device_id_type=MESH)

    load_left.wait()
    load_right.wait()
    left = [lv[k].astype(F32) for k in range(2)]
    right = jnp.concatenate([rv[k].astype(F32) for k in range(2)], axis=0)
    full = 2 * half
    for h in range(2):
        cut = [part[:, h * half:(h + 1) * half] for part in left]
        a_own[h] = jnp.concatenate(cut + [jnp.zeros((12, half), F32)], axis=0).astype(BF16)
    b_own[...] = jnp.concatenate([right, jnp.zeros((12, width), F32)], axis=0).astype(BF16)
    r_own[...] = jnp.concatenate(
        [right[:, b * 128:(b + 1) * 128] for b in range(width // 128)], axis=0
    ).astype(BF16)
    member = lax.broadcasted_iota(jnp.int32, (2, full), 0)
    weights = jnp.where(member == 0, fit[0], fit[1])
    weighted = jnp.concatenate([part * weights for part in left], axis=0)
    for q in range(16):
        l_own[q] = jnp.concatenate(
            [weighted[:, (2 * q + c) * 128:(2 * q + c + 1) * 128] for c in range(2)], axis=0
        )
    av[16:, :] = jnp.zeros((av.shape[0] - 16, half), BF16)

    @pl.when(stays)
    def _():
        av[:16, :] = a_own[core]
        bv[...] = b_own[...]

    l1[0] = l_own[pl.ds(4 * x, 4)]
    r1[0] = r_own[...]
    pl.semaphore_wait(barrier, len(peers))

    quarter = half // 4
    sub = quarter // SUBS
    edge = (zl == 0) | (zl == 3)
    inner = (zl == 1) | (zl == 2)
    lag = jnp.where(edge, 0, 1)
    outward = jnp.where(zl == 3, 1, 7)
    z_cross = device(x, y, mod(z + outward, 8), core)
    z_inward = device(x, y, mod(z + 8 - outward, 8), core)

    def piece(n, owner, base=0):
        start = base + owner * quarter + lax.rem(n, SUBS) * sub
        return pl.ds(pl.multiple_of(start, sub), sub)

    def held(n, owner, side):
        return wt.at[(n // SUBS) * 2 + side, piece(n, owner)]

    def weight_start(n):
        remote(
            (wr_hbm, wo_hbm)[n // SUBS].at[piece(n, x, core * half)], held(n, x, zh),
            wz_s.at[n, 0], wz_r.at[n], z_cross, edge,
        )

    def weight_send(place, n, which, target):
        return pltpu.make_async_remote_copy(
            src_ref=place, dst_ref=place, send_sem=wx_s.at[n, which],
            recv_sem=wx_r.at[n, which], device_id=target, device_id_type=MESH,
        )

    def weight_inward(place, n):
        return pltpu.make_async_remote_copy(
            src_ref=place, dst_ref=place, send_sem=wz_s.at[n, 1],
            recv_sem=wz_r.at[n], device_id=z_inward, device_id_type=MESH,
        )

    def weight_slot(slot):
        n = slot - lag

        @pl.when((n >= 0) & (n < 2 * SUBS))
        def _():
            place = held(n, x, 1 - zh)
            arrived(place, wz_r.at[n])
            pl.when(edge)(weight_inward(place, n).start)
            weight_send(place, n, 0, x_up).start()
            weight_send(place, n, 1, x_down).start()

        m = n - 2

        @pl.when((m >= 0) & (m < 2 * SUBS))
        def _():
            odd = lax.rem(m, 2)
            place = held(m, mod(x + 3 - 2 * odd, 4), 1 - zh)
            arrived(place, wx_r.at[m, odd])
            weight_send(place, m, 2, device(mod(x + 1 + 2 * odd, 4), y, z, core)).start()

    def weight_done(w):
        for n in range(w * SUBS, (w + 1) * SUBS):
            odd = n % 2
            arrived(held(n, mod(x + 1 + 2 * odd, 4), 1 - zh), wx_r.at[n, 1 - odd])
            arrived(held(n, mod(x + 2, 4), 1 - zh), wx_r.at[n, 2])

    def weight_sent():
        for n in range(2 * SUBS):
            place = held(n, x, 1 - zh)
            pl.when(edge)(weight_inward(place, n).wait_send)
            for which in range(3):
                weight_send(place, n, which, x_up).wait_send()

    def spread(buf, k, send, recv, when=None):
        place = buf.at[chunk(k), mine]
        remote(place, place, send.at[k, 0], recv.at[k, 0], up, when)
        remote(place, place, send.at[k, 1], recv.at[k, 1], down, when)

    def relay(buf, k, send, recv, when=None):
        def ready(place, sem):
            if when is None:
                arrived(place, sem)
            else:
                pl.when(when)(lambda: arrived(place, sem))

        ready(buf.at[chunk(k), below], recv.at[k, 0])
        place = buf.at[chunk(k, 0), below]
        remote(place, place, send.at[k, 2], recv.at[k, 2], up, when)
        ready(buf.at[chunk(k), above], recv.at[k, 1])
        place = buf.at[chunk(k, 1), above]
        remote(place, place, send.at[k, 3], recv.at[k, 3], down, when)

    def gathered(buf, k, recv):
        arrived(buf.at[chunk(k, 0), far], recv.at[k, 2])
        arrived(buf.at[chunk(k, 1), far], recv.at[k, 3])

    def x_ready(k, when):
        if when is stays:
            pl.when(stays)(load_x[k].wait)
        else:
            pl.when(mover)(lambda: arrived(xg.at[chunk(k), mine], swap_r.at[0, k]))
        spread(xg, k, xy_s, xy_r, when)

    def part(which, buf, k, side, sender, fresh):
        slot = which * CHUNKS + k
        value = buf[chunk(k), :]
        product = jnp.dot(value, wt[2 * which + side], preferred_element_type=F32)
        if fresh:
            proj[which, chunk(k), :] = lax.dot_general(
                value, av[...], (((1,), (1,)), ((), ())), preferred_element_type=F32
            )
        send = pltpu.make_async_remote_copy(
            src_ref=part_out.at[slot], dst_ref=part_in.at[slot],
            send_sem=part_s.at[slot], recv_sem=part_r.at[slot],
            device_id=twin, device_id_type=MESH,
        )
        pending.append((sender, send))

        @pl.when(sender)
        def _():
            part_out[slot, :, :width] = product
            part_out[slot, :, width:] = proj[which, chunk(k), :]
            send.start()

        @pl.when(jnp.logical_not(sender))
        def _():
            keep[slot] = product

    def total(which, k):
        at = which * 2 + k // (CHUNKS // 2)
        slot = which * CHUNKS + k
        arrived(part_in.at[slot], part_r.at[slot])
        scaled = noise_scale * (proj[which, chunk(k), :] + part_in[slot, :, width:])
        return (
            keep[slot] + part_in[slot, :, :width]
            + scaled[:, at:at + 1] * bv[at:at + 1, :].astype(F32)
        )

    def gate(k):
        gated = jax.nn.sigmoid(total(0, k)) * ro[chunk(k), :].astype(F32)
        gg[chunk(k), mine] = gated.astype(BF16)

    def a_part(k):
        gathered(xg, k, xy_r)
        if k == 0:
            load_wr.wait()
        part(0, xg, k, zh, mover, True)

    def a_finish(k):
        @pl.when(stays)
        def _():
            if k == 0:
                load_ro.wait()
            gate(k)

        spread(gg, k, gy_s, gy_r, stays)

    def b_part(k):
        part(0, xg, k, 1 - zh, stays, False)

    def b_finish(k):
        @pl.when(mover)
        def _():
            arrived(ro.at[chunk(k)], swap_r.at[1, k])
            gate(k)

        spread(gg, k, gy_s, gy_r, mover)

    store = []

    def c_part(k):
        gathered(gg, k, gy_r)
        part(1, gg, k, 1 - zh, stays, True)

    def c_finish(k):
        @pl.when(mover)
        def _():
            outs[chunk(k), :] = total(1, k).astype(BF16)

        remote(
            outs.at[chunk(k)], out_hbm.at[chunk(k)],
            swap_s.at[2, k], swap_r.at[2, k], partner, mover,
        )

    def d_part(k):
        part(1, gg, k, zh, mover, False)

    def d_finish(k):
        @pl.when(stays)
        def _():
            outs[chunk(k), :] = total(1, k).astype(BF16)

        store.append(local_copy(outs.at[chunk(k)], out_hbm.at[chunk(k)], load.at[16 + CHUNKS + k], stays))

    def estimate_one():
        for d in range(3):
            remote(
                l_own.at[pl.ds(4 * mod(x + d + 1, 4), 4)], l1.at[d + 1],
                e1_s.at[0, d], e1_r.at[0, d], x_peer[d],
            )
            remote(r_own, r1.at[d + 1], e1_s.at[1, d], e1_r.at[1, d], x_peer[d])

    def estimate_two():
        for d in range(3):
            arrived(l1.at[d + 1], e1_r.at[0, d])
            arrived(r1.at[d + 1], e1_r.at[1, d])
        for d in range(3):
            remote(
                l1.at[:, mod(zl + d + 1, 4)], l2.at[d + 1],
                e2_s.at[0, d], e2_r.at[0, d], zl_peer[d],
            )
            remote(r1, r2.at[d + 1], e2_s.at[1, d], e2_r.at[1, d], zl_peer[d])
        l2[0] = l1[:, zl]
        r2[0] = r1[...]

    def estimate_three():
        for d in range(3):
            arrived(l2.at[d + 1], e2_r.at[0, d])
            arrived(r2.at[d + 1], e2_r.at[1, d])
        remote(l2, l3, e3_s.at[0], e3_r.at[0], twin)
        remote(r2, r3, e3_s.at[1], e3_r.at[1], twin)

    def estimate_sum():
        arrived(l3, e3_r.at[0])
        arrived(r3, e3_r.at[1])
        n = 16
        lrow = lax.broadcasted_iota(jnp.int32, (n * 8, n * 16), 0)
        rrow = lax.broadcasted_iota(jnp.int32, (n * 8, n * 16), 1)
        same = (lrow // 8 == rrow // 16) & (lrow % 8 == core * 4 + rrow % 4)
        pick = jnp.where(same, 1.0, 0.0).astype(BF16)
        block = (lax.broadcasted_iota(jnp.int32, (n * 16, 128), 0) % 16) // 4
        which = (lax.broadcasted_iota(jnp.int32, (n * 8, width), 0) // 2) % 2
        sums = [None, None]
        for left, right in ((l2, r2), (l3, r3)):
            lt = left[...].reshape(n * 8, 128).T
            rt = right[...].reshape(n * 16, 128).astype(F32)
            wide = jnp.concatenate(
                [jnp.where(block == b, rt, 0.0).astype(BF16) for b in range(width // 128)], axis=1
            )
            chosen = jnp.dot(pick, wide, preferred_element_type=F32)
            high = lt.astype(BF16)
            rest = lt - high.astype(F32)
            middle = rest.astype(BF16)
            low = (rest - middle.astype(F32)).astype(BF16)
            for k in range(2):
                operand = jnp.where(which == k, chosen, 0.0).astype(BF16)
                for piece in (low, middle, high):
                    term = jnp.dot(piece, operand, preferred_element_type=F32)
                    sums[k] = term if sums[k] is None else sums[k] + term
        for k in range(2):
            est[k] = sums[k]
        store.append(local_copy(est, est_hbm, load.at[15]))

    def x_swap(k):
        remote(
            x_hbm.at[chunk(k)], xg.at[chunk(k), mine],
            swap_s.at[0, k], swap_r.at[0, k], partner, mover,
        )

    def ro_swap(k):
        remote(
            ro_hbm.at[chunk(k)], ro.at[chunk(k)],
            swap_s.at[1, k], swap_r.at[1, k], partner, mover,
        )

    def x_relay(k, when):
        relay(xg, k, xy_s, xy_r, when)

    def g_relay(k, when):
        relay(gg, k, gy_s, gy_r, when)

    x_ready(0, stays)
    x_relay(0, stays)
    x_swap(0)
    weight_start(0)
    x_ready(1, stays)
    weight_start(1)
    x_swap(1)
    x_ready(0, mover)
    weight_start(2)
    weight_start(3)
    x_ready(2, stays)
    x_relay(1, stays)

    remote(b_own, bv, swap_s.at[3, 0], swap_r.at[3, 0], partner, mover)
    remote(
        a_own.at[1 - core], av.at[pl.ds(0, 16)],
        swap_s.at[3, 1], swap_r.at[3, 1], twin, stays,
    )
    estimate_one()
    weight_slot(0)
    x_swap(2)
    weight_start(4)
    x_relay(2, stays)
    x_ready(3, stays)
    x_relay(0, mover)
    weight_start(5)
    weight_slot(1)

    @pl.when(mover)
    def _():
        arrived(av.at[pl.ds(0, 16)], swap_r.at[3, 1])
        arrived(bv, swap_r.at[3, 0])

    a_part(0)
    weight_slot(2)
    x_ready(1, mover)
    estimate_two()
    weight_slot(3)
    weight_start(6)
    x_ready(2, mover)
    x_relay(1, mover)
    x_swap(3)
    a_finish(0)
    weight_slot(4)
    x_relay(2, mover)
    weight_slot(5)
    estimate_three()
    weight_slot(6)
    a_part(1)
    weight_start(7)
    a_finish(1)
    x_ready(3, mover)
    g_relay(0, stays)
    ro_swap(0)
    ro_swap(1)
    weight_done(0)
    x_relay(3, stays)
    weight_slot(7)
    x_relay(3, mover)
    b_part(0)
    g_relay(1, stays)
    a_part(2)
    b_part(1)
    b_finish(0)
    weight_slot(8)
    a_finish(2)
    a_part(3)
    b_part(2)
    ro_swap(2)
    ro_swap(3)
    weight_slot(9)
    b_finish(1)
    weight_slot(10)
    g_relay(0, mover)
    b_part(3)
    g_relay(1, mover)
    g_relay(2, stays)
    load_wo.wait()
    weight_done(1)
    b_finish(2)
    estimate_sum()
    c_part(0)
    c_finish(0)
    a_finish(3)
    b_finish(3)
    c_part(1)
    g_relay(3, stays)
    c_finish(1)
    d_part(0)
    g_relay(2, mover)
    g_relay(3, mover)
    d_part(1)
    c_part(2)
    d_finish(0)
    c_finish(2)
    d_part(2)
    c_part(3)
    c_finish(3)
    d_part(3)
    d_finish(1)
    d_finish(2)
    d_finish(3)

    for copy in store[:1]:
        copy.wait()

    @pl.when(stays)
    def _():
        for copy in store[1:]:
            copy.wait()

    @pl.when(mover)
    def _():
        for k in range(CHUNKS):
            arrived(out_hbm.at[chunk(k)], swap_r.at[2, k])

    weight_sent()
    for when, copy in pending:
        if when is None:
            copy.wait_send()
        else:
            pl.when(when)(copy.wait_send)


def local(inputs, readout, recept_weight, output_weight, left_vectors, right_vectors, fitness):
    members, seq_len, width = inputs.shape
    full = left_vectors.shape[2]
    rows, half = members * seq_len, full // 2
    step = rows // CHUNKS
    anywhere = pl.BlockSpec(memory_space=pl.ANY)
    dma = pltpu.SemaphoreType.DMA
    outputs, estimate = pl.pallas_call(
        kernel,
        name="es_step",
        out_shape=(
            jax.ShapeDtypeStruct((rows, width), BF16),
            jax.ShapeDtypeStruct((2, 128, width), F32),
        ),
        in_specs=[anywhere] * 6 + [pl.BlockSpec(memory_space=pltpu.SMEM)],
        out_specs=(anywhere, anywhere),
        scratch_shapes=[
            pltpu.VMEM((rows, half), BF16),
            pltpu.VMEM((rows, half), BF16),
            pltpu.VMEM((rows, width), BF16),
            pltpu.VMEM((4, half, width), BF16),
            pltpu.VMEM((128, half), BF16),
            pltpu.VMEM((16, width), BF16),
            pltpu.VMEM((2, rows, 128), F32),
            pltpu.VMEM((2 * CHUNKS, step, width + 128), F32),
            pltpu.VMEM((2 * CHUNKS, step, width + 128), F32),
            pltpu.VMEM((2 * CHUNKS, step, width), F32),
            pltpu.VMEM((rows, width), BF16),
            pltpu.VMEM((2, members, full), BF16),
            pltpu.VMEM((2, members, width), BF16),
            pltpu.VMEM((2, 16, half), BF16),
            pltpu.VMEM((16, width), BF16),
            pltpu.VMEM((16, 8, 128), F32),
            pltpu.VMEM((16, 128), BF16),
            pltpu.VMEM((4, 4, 8, 128), F32),
            pltpu.VMEM((4, 16, 128), BF16),
            pltpu.VMEM((4, 4, 8, 128), F32),
            pltpu.VMEM((4, 4, 16, 128), BF16),
            pltpu.VMEM((4, 4, 8, 128), F32),
            pltpu.VMEM((4, 4, 16, 128), BF16),
            pltpu.VMEM((2, 128, width), F32),
            dma((CHUNKS, 4)), dma((CHUNKS, 4)), dma((CHUNKS, 4)), dma((CHUNKS, 4)),
            dma((4, CHUNKS)), dma((4, CHUNKS)),
            dma((2 * SUBS, 2)), dma((2 * SUBS,)),
            dma((2 * SUBS, 3)), dma((2 * SUBS, 3)),
            dma((16 + 2 * CHUNKS,)),
            dma((2 * CHUNKS,)), dma((2 * CHUNKS,)),
            dma((2, 3)), dma((2, 3)), dma((2, 3)), dma((2, 3)),
            dma((2,)), dma((2,)),
        ],
        compiler_params=pltpu.CompilerParams(
            collective_id=0, has_side_effects=True, vmem_limit_bytes=56 * 1024 * 1024
        ),
    )(
        inputs.reshape(rows, width), readout.reshape(rows, width),
        recept_weight, output_weight, left_vectors, right_vectors, fitness,
    )
    return outputs.reshape(members, seq_len, width), estimate * (1.0 / (noise_scale * 64))


def solution(mesh):
    return jax.shard_map(
        local,
        mesh=mesh,
        in_specs=(
            P("pop", None, "tensor"),
            P("pop", None, "tensor"),
            P(None, "tensor"),
            P(None, "tensor"),
            P(None, "pop", None),
            P(None, "pop", "tensor"),
            P("pop"),
        ),
        out_specs=(P("pop", None, "tensor"), P(None, "pop", "tensor")),
        check_vma=False,
    )
```

```python
import jax
import jax.numpy as jnp
from jax import lax
from jax.experimental import pallas as pl
from jax.experimental.pallas import tpu as pltpu
from jax.sharding import PartitionSpec as P

MESH = pl.DeviceIdType.MESH
noise_scale = 0.02
CHUNKS = 4
SUBS = 4
F32 = jnp.float32
BF16 = jnp.bfloat16


def mod(value, size):
    return lax.rem(value + size, size)


def device(x, y, z, core):
    return ((x * 4 + lax.rem(z, 4)) * 2 + core, (z // 4) * 4 + y)


def kernel(
    x_hbm, ro_hbm, wr_hbm, wo_hbm, left_hbm, right_hbm, fit,
    out_hbm, est_hbm,
    xg, gg, ro, wt, av, bv, proj, part_out, part_in, keep, outs,
    lv, rv, a_own, b_own, l_own, r_own, l1, r1, l2, r2, l3, r3, est,
    xy_s, xy_r, gy_s, gy_r, swap_s, swap_r, wz_s, wz_r, wx_s, wx_r,
    load, part_s, part_r, e1_s, e1_r, e2_s, e2_r, e3_s, e3_r,
):
    pop, tensor = lax.axis_index("pop"), lax.axis_index("tensor")
    x, zl, core = pop // 8, lax.rem(pop // 2, 4), lax.rem(pop, 2)
    zh, y = tensor // 4, lax.rem(tensor, 4)
    z = zh * 4 + zl
    rows, width = ro.shape
    half = xg.shape[1]
    halfquarter = half // 8
    step = rows // CHUNKS
    mover = core != zh
    stays = core == zh

    up, down = device(x, mod(y + 1, 4), z, core), device(x, mod(y + 3, 4), z, core)
    partner = device(x, y, mod(z + 4, 8), 1 - core)
    twin = device(x, y, z, 1 - core)
    z_next = (device(x, y, mod(z + 7, 8), core), device(x, y, mod(z + 1, 8), core))
    x_peer = [device(mod(x + d, 4), y, z, core) for d in range(1, 4)]
    x_up, x_down = x_peer[0], x_peer[2]
    zl_peer = [device(x, y, zh * 4 + mod(zl + d, 4), core) for d in range(1, 4)]
    z_near = [device(x, y, mod(z + d, 8), core) for d in (1, 2, 3, 5, 6, 7)]

    pending = []

    def remote(src, dst, send, recv, target, when=None):
        copy = pltpu.make_async_remote_copy(
            src_ref=src, dst_ref=dst, send_sem=send, recv_sem=recv,
            device_id=target, device_id_type=MESH,
        )
        pending.append((when, copy))
        if when is None:
            copy.start()
        else:
            pl.when(when)(copy.start)

    def arrived(dst, recv):
        pltpu.make_async_remote_copy(
            src_ref=dst, dst_ref=dst, send_sem=recv, recv_sem=recv,
            device_id=twin, device_id_type=MESH,
        ).wait_recv()

    def chunk(k, part=None):
        if part is None:
            return pl.ds(k * step, step)
        return pl.ds(k * step + part * (step // 2), step // 2)

    def columns(which):
        return pl.ds(pl.multiple_of(which * width, width), width)

    mine = columns(y)
    below, above, far = columns(mod(y + 3, 4)), columns(mod(y + 1, 4)), columns(mod(y + 2, 4))
    my_half = pl.ds(pl.multiple_of(core * half, half), half)
    twin_half = pl.ds(pl.multiple_of((1 - core) * half, half), half)

    local = []

    def local_copy(src, dst, sem, when=None):
        copy = pltpu.make_async_copy(src, dst, sem)
        if when is None:
            copy.start()
        else:
            pl.when(when)(copy.start)
        return copy

    load_left = local_copy(left_hbm, lv, load.at[1])
    load_right = local_copy(right_hbm, rv, load.at[2])
    load_x = [
        local_copy(x_hbm.at[chunk(k)], xg.at[chunk(k), mine], load.at[16 + k], stays)
        for k in range(CHUNKS)
    ]
    load_wr = local_copy(wr_hbm.at[my_half], wt.at[zh], load.at[0])
    load_ro = local_copy(ro_hbm, ro, load.at[8], stays)
    load_wo = local_copy(wo_hbm.at[my_half], wt.at[2 + zh], load.at[3])

    barrier = pltpu.get_barrier_semaphore()
    peers = [up, down, partner, twin] + x_peer + z_near
    for peer in peers:
        pl.semaphore_signal(barrier, inc=1, device_id=peer, device_id_type=MESH)

    load_left.wait()
    load_right.wait()
    left = [lv[k].astype(F32) for k in range(2)]
    right = jnp.concatenate([rv[k].astype(F32) for k in range(2)], axis=0)
    full = 2 * half
    for h in range(2):
        cut = [part[:, h * half:(h + 1) * half] for part in left]
        a_own[h] = jnp.concatenate(cut + [jnp.zeros((12, half), F32)], axis=0).astype(BF16)
    b_own[...] = jnp.concatenate([right, jnp.zeros((12, width), F32)], axis=0).astype(BF16)
    r_own[...] = jnp.concatenate(
        [right[:, b * 128:(b + 1) * 128] for b in range(width // 128)], axis=0
    ).astype(BF16)
    member = lax.broadcasted_iota(jnp.int32, (2, full), 0)
    weights = jnp.where(member == 0, fit[0], fit[1])
    weighted = jnp.concatenate([part * weights for part in left], axis=0)
    for q in range(16):
        l_own[q] = jnp.concatenate(
            [weighted[:, (2 * q + c) * 128:(2 * q + c + 1) * 128] for c in range(2)], axis=0
        )
    av[16:, :] = jnp.zeros((av.shape[0] - 16, half), BF16)

    @pl.when(stays)
    def _():
        av[:16, :] = a_own[core]
        bv[...] = b_own[...]

    l1[0] = l_own[pl.ds(4 * x, 4)]
    r1[0] = r_own[...]
    pl.semaphore_wait(barrier, len(peers))

    quarter = half // 4
    sub = quarter // SUBS
    edge = (zl == 0) | (zl == 3)
    inner = (zl == 1) | (zl == 2)
    lag = jnp.where(edge, 0, 1)
    outward = jnp.where(zl == 3, 1, 7)
    z_cross = device(x, y, mod(z + outward, 8), core)
    z_inward = device(x, y, mod(z + 8 - outward, 8), core)

    def piece(n, owner, base=0):
        start = base + owner * quarter + lax.rem(n, SUBS) * sub
        return pl.ds(pl.multiple_of(start, sub), sub)

    def held(n, owner, side):
        return wt.at[(n // SUBS) * 2 + side, piece(n, owner)]

    def weight_start(n):
        remote(
            (wr_hbm, wo_hbm)[n // SUBS].at[piece(n, x, core * half)], held(n, x, zh),
            wz_s.at[n, 0], wz_r.at[n], z_cross, edge,
        )

    def weight_send(place, n, which, target):
        return pltpu.make_async_remote_copy(
            src_ref=place, dst_ref=place, send_sem=wx_s.at[n, which],
            recv_sem=wx_r.at[n, which], device_id=target, device_id_type=MESH,
        )

    def weight_inward(place, n):
        return pltpu.make_async_remote_copy(
            src_ref=place, dst_ref=place, send_sem=wz_s.at[n, 1],
            recv_sem=wz_r.at[n], device_id=z_inward, device_id_type=MESH,
        )

    def weight_slot(slot):
        n = slot - lag

        @pl.when((n >= 0) & (n < 2 * SUBS))
        def _():
            place = held(n, x, 1 - zh)
            arrived(place, wz_r.at[n])
            pl.when(edge)(weight_inward(place, n).start)
            weight_send(place, n, 0, x_up).start()
            weight_send(place, n, 1, x_down).start()

        m = n - 2

        @pl.when((m >= 0) & (m < 2 * SUBS))
        def _():
            odd = lax.rem(m, 2)
            place = held(m, mod(x + 3 - 2 * odd, 4), 1 - zh)
            arrived(place, wx_r.at[m, odd])
            weight_send(place, m, 2, device(mod(x + 1 + 2 * odd, 4), y, z, core)).start()

    def weight_done(w):
        for n in range(w * SUBS, (w + 1) * SUBS):
            odd = n % 2
            arrived(held(n, mod(x + 1 + 2 * odd, 4), 1 - zh), wx_r.at[n, 1 - odd])
            arrived(held(n, mod(x + 2, 4), 1 - zh), wx_r.at[n, 2])

    def weight_sent():
        for n in range(2 * SUBS):
            place = held(n, x, 1 - zh)
            pl.when(edge)(weight_inward(place, n).wait_send)
            for which in range(3):
                weight_send(place, n, which, x_up).wait_send()

    def spread(buf, k, send, recv, when=None):
        place = buf.at[chunk(k), mine]
        remote(place, place, send.at[k, 0], recv.at[k, 0], up, when)
        remote(place, place, send.at[k, 1], recv.at[k, 1], down, when)

    def relay(buf, k, send, recv, when=None):
        def ready(place, sem):
            if when is None:
                arrived(place, sem)
            else:
                pl.when(when)(lambda: arrived(place, sem))

        ready(buf.at[chunk(k), below], recv.at[k, 0])
        place = buf.at[chunk(k, 0), below]
        remote(place, place, send.at[k, 2], recv.at[k, 2], up, when)
        ready(buf.at[chunk(k), above], recv.at[k, 1])
        place = buf.at[chunk(k, 1), above]
        remote(place, place, send.at[k, 3], recv.at[k, 3], down, when)

    def gathered(buf, k, recv):
        arrived(buf.at[chunk(k, 0), far], recv.at[k, 2])
        arrived(buf.at[chunk(k, 1), far], recv.at[k, 3])

    def x_ready(k, when):
        if when is stays:
            pl.when(stays)(load_x[k].wait)
        else:
            pl.when(mover)(lambda: arrived(xg.at[chunk(k), mine], swap_r.at[0, k]))
        spread(xg, k, xy_s, xy_r, when)

    def part(which, buf, k, side, sender, fresh):
        slot = which * CHUNKS + k
        value = buf[chunk(k), :]
        product = jnp.dot(value, wt[2 * which + side], preferred_element_type=F32)
        if fresh:
            proj[which, chunk(k), :] = lax.dot_general(
                value, av[...], (((1,), (1,)), ((), ())), preferred_element_type=F32
            )
        send = pltpu.make_async_remote_copy(
            src_ref=part_out.at[slot], dst_ref=part_in.at[slot],
            send_sem=part_s.at[slot], recv_sem=part_r.at[slot],
            device_id=twin, device_id_type=MESH,
        )
        pending.append((sender, send))

        @pl.when(sender)
        def _():
            part_out[slot, :, :width] = product
            part_out[slot, :, width:] = proj[which, chunk(k), :]
            send.start()

        @pl.when(jnp.logical_not(sender))
        def _():
            keep[slot] = product

    def total(which, k):
        at = which * 2 + k // (CHUNKS // 2)
        slot = which * CHUNKS + k
        arrived(part_in.at[slot], part_r.at[slot])
        scaled = noise_scale * (proj[which, chunk(k), :] + part_in[slot, :, width:])
        return (
            keep[slot] + part_in[slot, :, :width]
            + scaled[:, at:at + 1] * bv[at:at + 1, :].astype(F32)
        )

    def gate(k):
        gated = jax.nn.sigmoid(total(0, k)) * ro[chunk(k), :].astype(F32)
        gg[chunk(k), mine] = gated.astype(BF16)

    def a_part(k):
        gathered(xg, k, xy_r)
        if k == 0:
            load_wr.wait()
        part(0, xg, k, zh, mover, True)

    def a_finish(k):
        @pl.when(stays)
        def _():
            if k == 0:
                load_ro.wait()
            gate(k)

        spread(gg, k, gy_s, gy_r, stays)

    def b_part(k):
        part(0, xg, k, 1 - zh, stays, False)

    def b_finish(k):
        @pl.when(mover)
        def _():
            arrived(ro.at[chunk(k)], swap_r.at[1, k])
            gate(k)

        spread(gg, k, gy_s, gy_r, mover)

    store = []

    def c_part(k):
        gathered(gg, k, gy_r)
        part(1, gg, k, 1 - zh, stays, True)

    def c_finish(k):
        @pl.when(mover)
        def _():
            outs[chunk(k), :] = total(1, k).astype(BF16)

        remote(
            outs.at[chunk(k)], out_hbm.at[chunk(k)],
            swap_s.at[2, k], swap_r.at[2, k], partner, mover,
        )

    def d_part(k):
        part(1, gg, k, zh, mover, False)

    def d_finish(k):
        @pl.when(stays)
        def _():
            outs[chunk(k), :] = total(1, k).astype(BF16)

        store.append(local_copy(outs.at[chunk(k)], out_hbm.at[chunk(k)], load.at[16 + CHUNKS + k], stays))

    def estimate_one():
        for d in range(3):
            remote(
                l_own.at[pl.ds(4 * mod(x + d + 1, 4), 4)], l1.at[d + 1],
                e1_s.at[0, d], e1_r.at[0, d], x_peer[d],
            )
            remote(r_own, r1.at[d + 1], e1_s.at[1, d], e1_r.at[1, d], x_peer[d])

    def estimate_two():
        for d in range(3):
            arrived(l1.at[d + 1], e1_r.at[0, d])
            arrived(r1.at[d + 1], e1_r.at[1, d])
        for d in range(3):
            remote(
                l1.at[:, mod(zl + d + 1, 4)], l2.at[d + 1],
                e2_s.at[0, d], e2_r.at[0, d], zl_peer[d],
            )
            remote(r1, r2.at[d + 1], e2_s.at[1, d], e2_r.at[1, d], zl_peer[d])
        l2[0] = l1[:, zl]
        r2[0] = r1[...]

    def estimate_three():
        for d in range(3):
            arrived(l2.at[d + 1], e2_r.at[0, d])
            arrived(r2.at[d + 1], e2_r.at[1, d])
        remote(l2, l3, e3_s.at[0], e3_r.at[0], twin)
        remote(r2, r3, e3_s.at[1], e3_r.at[1], twin)

    def estimate_sum():
        arrived(l3, e3_r.at[0])
        arrived(r3, e3_r.at[1])
        n = 16
        lrow = lax.broadcasted_iota(jnp.int32, (n * 8, n * 16), 0)
        rrow = lax.broadcasted_iota(jnp.int32, (n * 8, n * 16), 1)
        same = (lrow // 8 == rrow // 16) & (lrow % 8 == core * 4 + rrow % 4)
        pick = jnp.where(same, 1.0, 0.0).astype(BF16)
        block = (lax.broadcasted_iota(jnp.int32, (n * 16, 128), 0) % 16) // 4
        which = (lax.broadcasted_iota(jnp.int32, (n * 8, width), 0) // 2) % 2
        sums = [None, None]
        for left, right in ((l2, r2), (l3, r3)):
            lt = left[...].reshape(n * 8, 128).T
            rt = right[...].reshape(n * 16, 128).astype(F32)
            wide = jnp.concatenate(
                [jnp.where(block == b, rt, 0.0).astype(BF16) for b in range(width // 128)], axis=1
            )
            chosen = jnp.dot(pick, wide, preferred_element_type=F32)
            high = lt.astype(BF16)
            rest = lt - high.astype(F32)
            middle = rest.astype(BF16)
            low = (rest - middle.astype(F32)).astype(BF16)
            for k in range(2):
                operand = jnp.where(which == k, chosen, 0.0).astype(BF16)
                for piece in (low, middle, high):
                    term = jnp.dot(piece, operand, preferred_element_type=F32)
                    sums[k] = term if sums[k] is None else sums[k] + term
        for k in range(2):
            est[k] = sums[k]
        store.append(local_copy(est, est_hbm, load.at[15]))

    def x_swap(k):
        remote(
            x_hbm.at[chunk(k)], xg.at[chunk(k), mine],
            swap_s.at[0, k], swap_r.at[0, k], partner, mover,
        )

    def ro_swap(k):
        remote(
            ro_hbm.at[chunk(k)], ro.at[chunk(k)],
            swap_s.at[1, k], swap_r.at[1, k], partner, mover,
        )

    def x_relay(k, when):
        relay(xg, k, xy_s, xy_r, when)

    def g_relay(k, when):
        relay(gg, k, gy_s, gy_r, when)

    x_ready(0, stays)
    x_relay(0, stays)
    x_swap(0)
    weight_start(0)
    x_ready(1, stays)
    weight_start(1)
    x_swap(1)
    x_ready(0, mover)
    weight_start(2)
    weight_start(3)
    x_ready(2, stays)
    x_relay(1, stays)

    remote(b_own, bv, swap_s.at[3, 0], swap_r.at[3, 0], partner, mover)
    remote(
        a_own.at[1 - core], av.at[pl.ds(0, 16)],
        swap_s.at[3, 1], swap_r.at[3, 1], twin, stays,
    )
    estimate_one()
    weight_slot(0)
    x_swap(2)
    weight_start(4)
    x_relay(2, stays)
    x_ready(3, stays)
    x_relay(0, mover)
    weight_start(5)
    weight_slot(1)

    @pl.when(mover)
    def _():
        arrived(av.at[pl.ds(0, 16)], swap_r.at[3, 1])
        arrived(bv, swap_r.at[3, 0])

    a_part(0)
    weight_slot(2)
    x_ready(1, mover)
    estimate_two()
    weight_slot(3)
    weight_start(6)
    x_ready(2, mover)
    x_relay(1, mover)
    x_swap(3)
    a_finish(0)
    weight_slot(4)
    x_relay(2, mover)
    weight_slot(5)
    estimate_three()
    weight_slot(6)
    a_part(1)
    weight_start(7)
    a_finish(1)
    x_ready(3, mover)
    g_relay(0, stays)
    ro_swap(0)
    ro_swap(1)
    weight_done(0)
    x_relay(3, stays)
    weight_slot(7)
    x_relay(3, mover)
    b_part(0)
    g_relay(1, stays)
    a_part(2)
    b_part(1)
    b_finish(0)
    weight_slot(8)
    a_finish(2)
    a_part(3)
    b_part(2)
    b_finish(1)
    ro_swap(2)
    ro_swap(3)
    weight_slot(9)
    g_relay(0, mover)
    weight_slot(10)
    b_part(3)
    g_relay(1, mover)
    g_relay(2, stays)
    load_wo.wait()
    weight_done(1)
    b_finish(2)
    estimate_sum()
    c_part(0)
    c_finish(0)
    a_finish(3)
    b_finish(3)
    c_part(1)
    g_relay(3, stays)
    c_finish(1)
    d_part(0)
    g_relay(2, mover)
    g_relay(3, mover)
    d_part(1)
    c_part(2)
    d_finish(0)
    c_finish(2)
    d_part(2)
    c_part(3)
    c_finish(3)
    d_part(3)
    d_finish(1)
    d_finish(2)
    d_finish(3)

    for copy in store[:1]:
        copy.wait()

    @pl.when(stays)
    def _():
        for copy in store[1:]:
            copy.wait()

    @pl.when(mover)
    def _():
        for k in range(CHUNKS):
            arrived(out_hbm.at[chunk(k)], swap_r.at[2, k])

    weight_sent()
    for when, copy in pending:
        if when is None:
            copy.wait_send()
        else:
            pl.when(when)(copy.wait_send)


def local(inputs, readout, recept_weight, output_weight, left_vectors, right_vectors, fitness):
    members, seq_len, width = inputs.shape
    full = left_vectors.shape[2]
    rows, half = members * seq_len, full // 2
    step = rows // CHUNKS
    anywhere = pl.BlockSpec(memory_space=pl.ANY)
    dma = pltpu.SemaphoreType.DMA
    outputs, estimate = pl.pallas_call(
        kernel,
        name="es_step",
        out_shape=(
            jax.ShapeDtypeStruct((rows, width), BF16),
            jax.ShapeDtypeStruct((2, 128, width), F32),
        ),
        in_specs=[anywhere] * 6 + [pl.BlockSpec(memory_space=pltpu.SMEM)],
        out_specs=(anywhere, anywhere),
        scratch_shapes=[
            pltpu.VMEM((rows, half), BF16),
            pltpu.VMEM((rows, half), BF16),
            pltpu.VMEM((rows, width), BF16),
            pltpu.VMEM((4, half, width), BF16),
            pltpu.VMEM((128, half), BF16),
            pltpu.VMEM((16, width), BF16),
            pltpu.VMEM((2, rows, 128), F32),
            pltpu.VMEM((2 * CHUNKS, step, width + 128), F32),
            pltpu.VMEM((2 * CHUNKS, step, width + 128), F32),
            pltpu.VMEM((2 * CHUNKS, step, width), F32),
            pltpu.VMEM((rows, width), BF16),
            pltpu.VMEM((2, members, full), BF16),
            pltpu.VMEM((2, members, width), BF16),
            pltpu.VMEM((2, 16, half), BF16),
            pltpu.VMEM((16, width), BF16),
            pltpu.VMEM((16, 8, 128), F32),
            pltpu.VMEM((16, 128), BF16),
            pltpu.VMEM((4, 4, 8, 128), F32),
            pltpu.VMEM((4, 16, 128), BF16),
            pltpu.VMEM((4, 4, 8, 128), F32),
            pltpu.VMEM((4, 4, 16, 128), BF16),
            pltpu.VMEM((4, 4, 8, 128), F32),
            pltpu.VMEM((4, 4, 16, 128), BF16),
            pltpu.VMEM((2, 128, width), F32),
            dma((CHUNKS, 4)), dma((CHUNKS, 4)), dma((CHUNKS, 4)), dma((CHUNKS, 4)),
            dma((4, CHUNKS)), dma((4, CHUNKS)),
            dma((2 * SUBS, 2)), dma((2 * SUBS,)),
            dma((2 * SUBS, 3)), dma((2 * SUBS, 3)),
            dma((16 + 2 * CHUNKS,)),
            dma((2 * CHUNKS,)), dma((2 * CHUNKS,)),
            dma((2, 3)), dma((2, 3)), dma((2, 3)), dma((2, 3)),
            dma((2,)), dma((2,)),
        ],
        compiler_params=pltpu.CompilerParams(
            collective_id=0, has_side_effects=True, vmem_limit_bytes=56 * 1024 * 1024
        ),
    )(
        inputs.reshape(rows, width), readout.reshape(rows, width),
        recept_weight, output_weight, left_vectors, right_vectors, fitness,
    )
    return outputs.reshape(members, seq_len, width), estimate * (1.0 / (noise_scale * 64))


def solution(mesh):
    return jax.shard_map(
        local,
        mesh=mesh,
        in_specs=(
            P("pop", None, "tensor"),
            P("pop", None, "tensor"),
            P(None, "tensor"),
            P(None, "tensor"),
            P(None, "pop", None),
            P(None, "pop", "tensor"),
            P("pop"),
        ),
        out_specs=(P("pop", None, "tensor"), P(None, "pop", "tensor")),
        check_vma=False,
    )
```
